128 devices in a mesh: segment: 2 (over core), fsdp: 32 (over x, y_lo, z), dp: 2 (over y_hi).
Axes of the slice: x: 4, y: 4 (y_hi: 2, y_lo: 2; y = y_hi * 2 + y_lo), z: 4, core: 2. Of those that a mesh axis runs over, the one named last changes fastest.
Arguments:
- hooks: bfloat16 [2, 4, 256, 64, 6144], P('segment', 'dp', 'fsdp'), may hold values from -6 to 6
- proj_weight: bfloat16 [2, 6144, 256], P('segment', 'fsdp'), may hold values from -0.078125 to 0.078125
- conv_weight: bfloat16 [2, 2, 2304, 256], P('segment', None, 'fsdp'), may hold values from -0.125 to 0.125
- head_weight: bfloat16 [3, 256], replicated, may hold values from -0.375 to 0.375
- light_color: float32 [25, 3], replicated, may hold values from 0.3 to 1.5
- illum: int32 [4, 4], P('dp'), may hold values from 0 to 24
- offsets: int32 [4, 4, 2], P('dp'), may hold values from 0 to 32
- photos: bfloat16 [4, 4, 3, 96, 96], P('dp'), may hold values from 0 to 10
Outputs:
- grad_proj: float32 [2, 6144, 256], P('segment', 'fsdp')
- grad_conv: float32 [2, 2, 2304, 256], P('segment', None, 'fsdp')
- grad_head: float32 [3, 256], replicated
- loss: float32 [], replicated
The draws below stay inside these ranges and needn't reach their ends.
All inputs are finite; a program needn't handle non-finite values.
Results may differ from the reference program's by a relative error of at most 0.018.
Values may be sent and summed in bfloat16 or wider, within the bound.
A program may use at most 128 MiB of HBM per device.

```python
import jax
import jax.numpy as jnp
from jax import lax

D = 6144
F = 256
GRID = 64
PHOTO = 96
LIGHTS = 25
CROPS = 4
MICROS = 4
N_SEGMENT = 2


def draw_photos(key, part):
    surface_key, column_key = jax.random.split(jax.random.fold_in(key, 7))
    shape = (MICROS, CROPS, 3, PHOTO, PHOTO)
    row_pos = (jnp.arange(PHOTO, dtype=jnp.float32) / (PHOTO - 1)).reshape(1, 1, 1, PHOTO, 1)
    column_gain = jnp.exp(jnp.log(10.0) * jax.random.uniform(column_key, (MICROS, CROPS, 1, 1, PHOTO), jnp.float32))
    surface = jnp.clip(0.05 + 0.02 * jax.random.normal(surface_key, shape, jnp.float32), 0.0, 0.1)
    row_gain = jnp.exp(jnp.log(10.0) * row_pos)
    return jnp.clip(surface * row_gain * column_gain, 0.0, 10.0).astype(jnp.bfloat16)


def touch_ends(values, rng, least, high):
    longest = values.shape.index(max(values.shape))
    spots = []
    for shift in (0, 1):
        where = [jax.random.randint(jax.random.fold_in(rng, axis), (), 0, length) for axis, length in enumerate(values.shape)]
        where[longest] = (where[longest] + shift) % values.shape[longest]
        spots.append(tuple(where))
    return values.at[spots[0]].set(least).at[spots[1]].set(high)


def raised(array, own_key, source, target, shards_of, factor):
    owner, partner = [(jnp.arange(array.shape[dim]) // (array.shape[dim] // shards_of)).reshape([-1 if axis == dim else 1 for axis in range(array.ndim)]) for dim in (source, target)]
    chosen = jax.random.permutation(own_key, shards_of)[partner]
    strong = (owner == chosen) | (owner == (partner + shards_of // 2) % shards_of)
    return jnp.where(strong, factor * array, array)


def block_scale(own_key, extent, cuts, low, largest):
    level = 1.0
    for position, parts in cuts:
        steps = jax.random.uniform(jax.random.fold_in(jax.random.fold_in(own_key, 6), position), (parts,), jnp.float32, low / len(cuts), largest / len(cuts))
        level = level * jnp.repeat(jnp.exp(steps), extent[position] // parts).reshape((-1,) + (1,) * (len(extent) - 1 - position))
    return level


def centred(own_key, extent, width, limit, cuts=(), kind=jnp.bfloat16):
    drawn = width * jax.random.normal(own_key, extent, jnp.float32)
    if cuts:
        drawn = drawn * block_scale(own_key, extent, cuts, -0.22, 0.18)
    return jnp.clip(drawn, -limit, limit).astype(kind)


def gaussian_with(own_key, extent, scale, bound, cuts, heavy, held_as=jnp.bfloat16):
    values = scale * jax.random.normal(own_key, extent, jnp.float32)
    if cuts:
        values = values * block_scale(own_key, extent, cuts, -0.22, 0.18)
    return jnp.clip(raised(values, jax.random.fold_in(own_key, 3), *heavy), -bound, bound).astype(held_as)


def setup_inputs(seed: int = 0) -> dict:
    seeds = jax.random.split(jax.random.key(seed), 9)
    return {
        "hooks": gaussian_with(seeds[0], (N_SEGMENT, MICROS, CROPS * GRID, GRID, D), 1.0, 6.0, ((0, 2), (1, 2), (2, 32)), (2, 4, 32, 2.75)),
        "proj_weight": centred(seeds[1], (N_SEGMENT, D, F), D ** -0.5, 0.078125, ((0, 2), (1, 32))),
        "conv_weight": centred(seeds[2], (N_SEGMENT, 2, 9 * F, F), (9 * F) ** -0.5, 0.125, ((0, 2), (2, 32))),
        "head_weight": centred(seeds[3], (3, F), F ** -0.5, 0.375),
        "light_color": jnp.clip(jax.random.uniform(seeds[4], (LIGHTS, 3), jnp.float32, 0.3, 1.5), 0.3, 1.5),
        "illum": touch_ends(jax.random.randint(seeds[5], (MICROS, CROPS), 0, LIGHTS), jax.random.fold_in(seeds[5], 1), 0, LIGHTS - 1).astype(jnp.int32),
        "offsets": touch_ends(jax.random.randint(seeds[6], (MICROS, CROPS, 2), 0, PHOTO - GRID + 1), jax.random.fold_in(seeds[6], 1), 0, PHOTO - GRID).astype(jnp.int32),
        "photos": draw_photos(jax.random.fold_in(seeds[8], 71), 0),
    }


LOSS_SCALE = 8192.0

def activate(values):
    return jax.nn.gelu(values, approximate=True)

def activate_slope(values):
    return jax.vjp(activate, values)[1](jnp.ones_like(values))[0]

def patches(field):
    rows_here, cols_here, channels = (field.shape[1], field.shape[2], field.shape[3])
    padded = jnp.pad(field, ((0, 0), (1, 1), (1, 1), (0, 0)))
    pieces = [padded[:, i:i + rows_here, j:j + cols_here, :] for i in range(3) for j in range(3)]
    return jnp.concatenate(pieces, axis=-1).reshape(-1, 9 * channels)

def contract_rows(left, right):
    return lax.dot_general(left, right, (((0,), (0,)), ((), ())), preferred_element_type=jnp.float32)

def flipped(kernel):
    channels = kernel.shape[1]
    grid_form = kernel.reshape(3, 3, channels, channels)[::-1, ::-1]
    return jnp.swapaxes(grid_form, 2, 3).reshape(9 * channels, channels)

def section_parts(segment_in, first_conv, second_conv):
    channels = segment_in.shape[-1]
    first_in = activate(segment_in.astype(jnp.float32)).astype(jnp.bfloat16)
    first_patches = patches(first_in)
    hidden = jnp.dot(first_patches, first_conv, preferred_element_type=jnp.float32)
    second_in = activate(hidden).astype(jnp.bfloat16).reshape(segment_in.shape)
    second_patches = patches(second_in)
    update = jnp.dot(second_patches, second_conv, preferred_element_type=jnp.float32)
    output = (segment_in.reshape(-1, channels).astype(jnp.float32) + update).astype(jnp.bfloat16)
    return (output.reshape(segment_in.shape), first_patches, hidden, second_patches)

def section_back(segment_in, out_grad, first_conv, second_conv, first_flip, second_flip):
    channels = segment_in.shape[-1]
    output, first_patches, hidden, second_patches = section_parts(segment_in, first_conv, second_conv)
    out_rows = out_grad.reshape(-1, channels)
    second_grad = jnp.dot(patches(out_grad), second_flip, preferred_element_type=jnp.float32)
    hidden_grad = (second_grad * activate_slope(hidden)).astype(jnp.bfloat16)
    first_grad = jnp.dot(patches(hidden_grad.reshape(segment_in.shape)), first_flip, preferred_element_type=jnp.float32)
    slope = activate_slope(segment_in.reshape(-1, channels).astype(jnp.float32))
    in_grad = (out_rows.astype(jnp.float32) + first_grad * slope).astype(jnp.bfloat16).reshape(segment_in.shape)
    return (in_grad, contract_rows(first_patches, hidden_grad), contract_rows(second_patches, out_rows))

def head_loss(output, head_weight, tints, targets, factor):
    channels = output.shape[-1]
    out_rows = output.reshape(-1, channels)
    logits = lax.dot_general(head_weight, out_rows, (((1,), (1,)), ((), ())), preferred_element_type=jnp.float32)
    albedo = jax.nn.sigmoid(logits.reshape(targets.shape))
    tint = jnp.transpose(tints)[:, :, None, None]
    mismatch = albedo * tint - targets
    squares = jnp.sum(mismatch * mismatch)
    logit_grad = (factor * mismatch * tint * albedo * (1.0 - albedo)).astype(jnp.bfloat16).reshape(3, -1)
    head_grad = lax.dot_general(logit_grad, out_rows, (((1,), (0,)), ((), ())), preferred_element_type=jnp.float32)
    out_grad = lax.dot_general(logit_grad, head_weight, (((0,), (0,)), ((), ())), preferred_element_type=jnp.float32)
    return (squares, head_grad, out_grad.astype(jnp.bfloat16).reshape(output.shape))

def crop_tints(illum, light_color):
    lights = light_color.shape[0]
    onehot = (illum[..., None] == jnp.arange(lights, dtype=jnp.int32)).astype(jnp.float32)
    return jnp.dot(onehot.reshape(-1, lights), light_color, precision=lax.Precision.HIGHEST)

def crop_targets(photos, offsets, row_base, rows_here, cols_here):

    def one_crop(picture, offset):
        start = (jnp.zeros((), jnp.int32), (offset[0] + row_base).astype(jnp.int32), offset[1].astype(jnp.int32))
        return lax.dynamic_slice(picture, start, (3, rows_here, cols_here))
    cut = jax.vmap(jax.vmap(one_crop))(photos, offsets).astype(jnp.float32)
    return jnp.moveaxis(cut, 2, 0)

def reference(hooks, proj_weight, conv_weight, head_weight, light_color, illum, offsets, photos):
    segments, micros, grid_size = (hooks.shape[0], hooks.shape[1], hooks.shape[3])
    crops = hooks.shape[2] // grid_size
    model_width = hooks.shape[4]
    channels = proj_weight.shape[2]
    npix = 3 * micros * crops * grid_size * grid_size
    factor = 2.0 * LOSS_SCALE / npix
    tints = crop_tints(illum, light_color).reshape(micros, crops, 3)
    targets = crop_targets(photos, offsets, jnp.zeros((), jnp.int32), grid_size, grid_size)
    segment_inputs = []
    incoming = [None] * micros
    for s in range(segments):
        saved = []
        for m in range(micros):
            projected = jnp.dot(hooks[s, m].reshape(-1, model_width), proj_weight[s], preferred_element_type=jnp.float32).astype(jnp.bfloat16)
            if s == 0:
                segment_in = projected
            else:
                segment_in = (projected.astype(jnp.float32) + incoming[m].reshape(-1, channels).astype(jnp.float32)).astype(jnp.bfloat16)
            segment_in = segment_in.reshape(crops, grid_size, grid_size, channels)
            saved.append(segment_in)
            incoming[m] = section_parts(segment_in, conv_weight[s, 0], conv_weight[s, 1])[0]
        segment_inputs.append(saved)
    squares = jnp.zeros((), jnp.float32)
    head_grad = jnp.zeros((3, channels), jnp.float32)
    out_grads = []
    for m in range(micros):
        part_squares, part_head, out_grad = head_loss(incoming[m], head_weight, tints[m], targets[:, m], factor)
        squares = squares + part_squares
        head_grad = head_grad + part_head
        out_grads.append(out_grad)
    grad_proj = []
    grad_conv = []
    for s in reversed(range(segments)):
        first_flip = flipped(conv_weight[s, 0])
        second_flip = flipped(conv_weight[s, 1])
        proj_sum = jnp.zeros((model_width, channels), jnp.float32)
        first_sum = jnp.zeros((9 * channels, channels), jnp.float32)
        second_sum = jnp.zeros((9 * channels, channels), jnp.float32)
        for m in range(micros):
            in_grad, first_part, second_part = section_back(segment_inputs[s][m], out_grads[m], conv_weight[s, 0], conv_weight[s, 1], first_flip, second_flip)
            proj_sum = proj_sum + contract_rows(hooks[s, m].reshape(-1, model_width), in_grad.reshape(-1, channels))
            first_sum = first_sum + first_part
            second_sum = second_sum + second_part
            out_grads[m] = in_grad
        grad_proj.insert(0, proj_sum)
        grad_conv.insert(0, jnp.stack([first_sum, second_sum]))
    return (jnp.stack(grad_proj), jnp.stack(grad_conv), head_grad, squares / npix)
```

```python
import functools

import jax
import jax.numpy as jnp
from jax import lax
from jax.experimental import pallas as pl
from jax.experimental.pallas import tpu as pltpu
from jax.sharding import PartitionSpec as P

LOSS_SCALE = 8192.0
MESH = pl.DeviceIdType.MESH
BF = jnp.bfloat16
F32 = jnp.float32

MICROS, ROWS, COLS, CH = 2, 8, 64, 256
TOKENS = MICROS * ROWS * COLS
HALF = ROWS * COLS
D = 6144
SLOT = 192
CSLOT = 72
CHUNK = 4 * SLOT

ORDER = [(0, 0), (0, 1), (-1, 0), (1, 0), (-1, 1), (1, 1), (2, 0), (2, 1)]
BACK = [(2, 0), (2, 1), (-1, 0), (1, 1), (1, 0), (-1, 1), (0, 1), (0, 0)]


def place():
    f = lax.axis_index("fsdp")
    return f // 8, (f // 4) % 2, f % 4


def at(x, y, z):
    return {"fsdp": x * 8 + y * 4 + z}


def dot(a, b, dims=((1,), (0,))):
    return lax.dot_general(a, b, (dims, ((), ())), preferred_element_type=F32)


def gelu_parts(v):
    c = 0.7978845608028654
    t = jnp.tanh(c * (v + 0.044715 * (v * v * v)))
    return t


def gelu(v):
    return 0.5 * v * (1.0 + gelu_parts(v))


def gelu_slope(v):
    c = 0.7978845608028654
    t = gelu_parts(v)
    return 0.5 * (1.0 + t) + 0.5 * v * (1.0 - t * t) * (c * (1.0 + 3.0 * 0.044715 * (v * v)))


class Axis:
    def __init__(self, p_is_x):
        x, y, z = place()
        self.p_is_x = p_is_x
        self.p, self.y, self.q = (x, y, z) if p_is_x else (z, y, x)

    def coords(self, dp, r, dq):
        p = (self.p + (dp + 4)) % 4
        q = (self.q + (dq + 4)) % 4
        y = (self.y + r) % 2
        return (p, y, q) if self.p_is_x else (q, y, p)

    def slot(self, dp, r, dq):
        x, y, z = self.coords(dp, r, dq)
        return x * 8 + y * 4 + z

    def device(self, dp, r, dq):
        return at(*self.coords(dp, r, dq))


def rel(dp, r, dq):
    return ((dp % 4) * 2 + r) * 4 + dq % 4


class Gather:
    def __init__(self, axis, buf, send, recv):
        self.a, self.buf, self.send, self.recv = axis, buf, send, recv
        self.copies = []

    def put(self, dp, r, dq, to):
        tp, tr, tq = to
        a = self.a
        slot = a.slot(dp, r, dq)
        copy = pltpu.make_async_remote_copy(
            src_ref=self.buf.at[slot],
            dst_ref=self.buf.at[slot],
            send_sem=self.send.at[len(self.copies)],
            recv_sem=self.recv.at[rel(dp - tp, (r + tr) % 2, dq - tq)],
            device_id=a.device(tp, tr, tq),
            device_id_type=MESH,
        )
        copy.start()
        self.copies.append(copy)

    def await_(self, dp, r, dq):
        a = self.a
        slot = a.slot(dp, r, dq)
        pltpu.make_async_remote_copy(
            src_ref=self.buf.at[slot],
            dst_ref=self.buf.at[slot],
            send_sem=self.send.at[0],
            recv_sem=self.recv.at[rel(dp, r, dq)],
            device_id=a.device(0, 1, 0),
            device_id_type=MESH,
        ).wait_recv()

    def event(self, i):
        dp, r = ORDER[i]
        if i > 0:
            self.await_(dp, r, 0)
        if i == 0:
            self.put(0, 0, 0, (0, 1, 0))
        if dp == 0:
            self.put(0, r, 0, (1, 0, 0))
            self.put(0, r, 0, (-1, 0, 0))
        if (dp, r) == (-1, 0):
            self.put(dp, r, 0, (1, 0, 0))
        if (dp, r) == (1, 1):
            self.put(dp, r, 0, (-1, 0, 0))
        self.put(dp, r, 0, (0, 0, 1))
        self.put(dp, r, 0, (0, 0, -1))

    def onward(self, i):
        dp, r = ORDER[i]
        self.await_(dp, r, -1)
        if r == 0:
            self.put(dp, r, -1, (0, 0, 1))
        self.await_(dp, r, 1)
        if r == 1:
            self.put(dp, r, 1, (0, 0, -1))

    def last(self, i):
        dp, r = ORDER[i]
        self.await_(dp, r, 2)

    def drain(self):
        for copy in self.copies:
            copy.wait_send()


def entry_barrier(devices):
    barrier = pltpu.get_barrier_semaphore()
    for device in devices:
        pl.semaphore_signal(barrier, inc=1, device_id=device, device_id_type=MESH)
    pl.semaphore_wait(barrier, len(devices))


def shift_parts(v):
    n = v.shape[0]
    col = lax.broadcasted_iota(jnp.int32, v.shape, 0) % COLS
    before = jnp.where(col == 0, 0.0, pltpu.roll(v, 1, 0))
    after = jnp.where(col == COLS - 1, 0.0, pltpu.roll(v, n - 1, 0))
    return before.astype(BF), v.astype(BF), after.astype(BF)


def main_kernel(
    npix,
    factor,
    hooks_ref,
    proj_ref,
    conv_ref,
    head_ref,
    light_ref,
    illum_ref,
    offsets_ref,
    photos_ref,
    grad_ref,
    gconv_ref,
    total_ref,
    hooks_v,
    wproj,
    wconv,
    wf32,
    wbf,
    acc,
    section_in,
    inc,
    out,
    og_in,
    og,
    hidden,
    cat_a,
    cat_b,
    cat_c,
    x1t,
    x2t,
    hsend,
    hrecv,
    targets,
    head_pad,
    hsum,
    hgot,
    hfin,
    load_sem,
    psend,
    precv,
    csend,
    crecv,
    hs_sem,
    hr_sem,
    seg_s,
    seg_r,
    sum_s,
    sum_r,
):
    x, y, z = place()
    seg = lax.axis_index("segment")
    dpi = lax.axis_index("dp")
    band = y * 4 + z
    sibling = {"segment": 1 - seg}
    dp_peer = {"dp": 1 - dpi}
    up_j, down_j = (band + 7) % 8, (band + 1) % 8
    up = at(x, up_j // 4, up_j % 4)
    down = at(x, down_j // 4, down_j % 4)

    loads = []
    pa = Axis(True)
    for i, (dp, r) in enumerate(ORDER):
        xs, ys, _ = pa.coords(dp, r, 0)
        c = xs * 2 + ys
        start = pl.multiple_of(c * CHUNK, CHUNK)
        copy = pltpu.make_async_copy(
            hooks_ref.at[:, pl.ds(start, CHUNK)], hooks_v.at[i], load_sem.at[i]
        )
        copy.start()
        loads.append(copy)

    me = x * 8 + y * 4 + z
    wproj[me] = proj_ref[...]
    wconv[me] = conv_ref[...]

    z1 = at(x, y, z + 1 - 2 * (z % 2))
    z2 = at(x, y, (z + 2) % 4)
    x1 = at(x + 1 - 2 * (x % 2), y, z)
    x2 = at((x + 2) % 4, y, z)
    y1 = at(x, 1 - y, z)
    entry_barrier(
        [
            at((x + 1) % 4, y, z),
            at((x + 3) % 4, y, z),
            at(x, y, (z + 1) % 4),
            at(x, y, (z + 3) % 4),
            y1,
            z2,
            x2,
            up,
            down,
            sibling,
            dp_peer,
        ]
    )

    gp = Gather(pa, wproj, psend, precv)
    gc = Gather(Axis(False), wconv, csend, crecv)

    gp.event(0)
    gc.event(0)

    yy = lax.broadcasted_iota(jnp.int32, (96, HALF), 0)
    nn = lax.broadcasted_iota(jnp.int32, (96, HALF), 1)
    row8 = lax.broadcasted_iota(jnp.int32, (8, HALF), 0)
    for m in range(MICROS):
        oy = offsets_ref[m, x, 0]
        ox = offsets_ref[m, x, 1]
        pick_col = (yy == ox + nn % COLS).astype(F32).astype(BF)
        pick_row = yy == oy + band * ROWS + nn // COLS
        block = jnp.zeros((8, HALF), F32)
        for c in range(3):
            q = dot(photos_ref[m, x, c], pick_col)
            line = jnp.sum(jnp.where(pick_row, q, 0.0), axis=0, keepdims=True)
            block = jnp.where(row8 == c, line, block)
        targets[:, m * HALF : (m + 1) * HALF] = block
    head_pad[...] = jnp.zeros((8, CH), F32)
    head_pad[0:3, :] = head_ref[...].astype(F32)

    acc[...] = jnp.zeros_like(acc)

    def project(i):
        loads[i].wait()
        dp, r = ORDER[i]
        xs, ys, _ = pa.coords(dp, r, 0)
        base = xs * 8 + ys * 4
        w = wproj[pl.ds(base, 4)].reshape(CHUNK, CH)

        def step(t, _):
            rows = pl.ds(pl.multiple_of(t * 256, 256), 256)
            acc[rows, :] += dot(hooks_v[i, rows, :], w)
            return 0

        lax.fori_loop(0, TOKENS // 256, step, 0)

    for i in range(1, 8):
        gp.event(i)
        gc.event(i)
        gp.onward(i - 1)
        gc.onward(i - 1)
        if i >= 2:
            gp.last(i - 2)
            gc.last(i - 2)
            project(i - 2)
    gp.onward(7)
    gc.onward(7)
    gc.last(6)
    gc.last(7)

    def gather_rows(k, _):
        start = pl.multiple_of(k * CSLOT, 8)
        wf32[0, pl.ds(start, CSLOT), :] = wconv[k, 0].astype(F32)
        wf32[1, pl.ds(start, CSLOT), :] = wconv[k, 1].astype(F32)
        return 0

    lax.fori_loop(0, 32, gather_rows, 0)

    def to_bf(k, _):
        start = pl.multiple_of(k * CH, CH)
        wbf[0, pl.ds(start, CH), :] = wf32[0, pl.ds(start, CH), :].astype(BF)
        wbf[1, pl.ds(start, CH), :] = wf32[1, pl.ds(start, CH), :].astype(BF)
        return 0

    lax.fori_loop(0, 9, to_bf, 0)
    gp.last(6)
    project(6)
    gp.last(7)
    project(7)
    gp.drain()
    gc.drain()

    def seg_copy(src, dst, k):
        return pltpu.make_async_remote_copy(
            src_ref=src,
            dst_ref=dst,
            send_sem=seg_s.at[k],
            recv_sem=seg_r.at[k],
            device_id=sibling,
            device_id_type=MESH,
        )

    @pl.when(seg == 0)
    def _():
        section_in[...] = acc[...].astype(BF)

    @pl.when(seg == 1)
    def _():
        seg_copy(out, inc, 0).wait_recv()
        section_in[...] = (acc[...].astype(BF).astype(F32) + inc[...].astype(F32)).astype(BF)

    halo_copies = []

    def halo_start(e):
        pair = []
        for side, device in ((0, up), (1, down)):
            copy = pltpu.make_async_remote_copy(
                src_ref=hsend.at[e, side],
                dst_ref=hrecv.at[e, 1 - side],
                send_sem=hs_sem.at[e, side],
                recv_sem=hr_sem.at[e, 1 - side],
                device_id=device,
                device_id_type=MESH,
            )
            copy.start()
            pair.append(copy)
        halo_copies.extend(pair)

    def fill(cat, m, value):
        a, b, c = shift_parts(value)
        shape = (ROWS, COLS, CH)
        cat[m, 1 : 1 + ROWS, :, 0:CH] = a.reshape(shape)
        cat[m, 1 : 1 + ROWS, :, CH : 2 * CH] = b.reshape(shape)
        cat[m, 1 : 1 + ROWS, :, 2 * CH : 3 * CH] = c.reshape(shape)

    def edges(e, m, value):
        hsend[e, 0, m] = value[0:COLS].astype(BF)
        hsend[e, 1, m] = value[HALF - COLS : HALF].astype(BF)

    def halo_wait(e, cat):
        for copy in halo_copies[-2:]:
            copy.wait()
        for side, row, last in ((0, 0, 0), (1, ROWS + 1, 7)):
            for m in range(MICROS):
                v = hrecv[e, side, m].astype(F32)
                v = jnp.where(band == last, jnp.zeros_like(v), v)
                a, b, c = shift_parts(v)
                cat[m, row, :, 0:CH] = a
                cat[m, row, :, CH : 2 * CH] = b
                cat[m, row, :, 2 * CH : 3 * CH] = c

    def tokens_of(m):
        return slice(m * HALF, (m + 1) * HALF)

    def conv(cat, which, m):
        total = None
        for ky in range(3):
            left = cat[m, ky : ky + ROWS].reshape(HALF, 3 * CH)
            part = dot(left, wbf[which, ky * 3 * CH : (ky + 1) * 3 * CH, :])
            total = part if total is None else total + part
        return total

    def conv_back(cat, which, m):
        total = None
        for ky in range(3):
            for kx in range(3):
                left = cat[m, ky : ky + ROWS, :, kx * CH : (kx + 1) * CH].reshape(HALF, CH)
                k = (2 - ky) * 3 + 2 - kx
                part = dot(left, wbf[which, k * CH : (k + 1) * CH, :], ((1,), (1,)))
                total = part if total is None else total + part
        return total

    def conv_weight_grad(xt, cat, which):
        for ky in range(3):
            total = None
            for m in range(MICROS):
                right = cat[m, 2 - ky : 2 - ky + ROWS].reshape(HALF, 3 * CH)
                part = dot(xt[:, tokens_of(m)], right)
                total = part if total is None else total + part
            for kx in range(3):
                j = 2 - kx
                row = (3 * ky + kx) * CH
                gconv_ref[which, row : row + CH, :] = total[:, j * CH : (j + 1) * CH]

    for m in range(MICROS):
        first = gelu(section_in[tokens_of(m), :].astype(F32)).astype(BF).astype(F32)
        edges(0, m, first)
        fill(cat_a, m, first)
    halo_start(0)
    for m in range(MICROS):
        first = cat_a[m, 1 : 1 + ROWS, :, CH : 2 * CH].reshape(HALF, CH).astype(F32)
        x1t[:, tokens_of(m)] = first.T.astype(BF)
    halo_wait(0, cat_a)
    for m in range(MICROS):
        h = conv(cat_a, 0, m)
        hidden[tokens_of(m), :] = h
        second = gelu(h).astype(BF).astype(F32)
        edges(1, m, second)
        fill(cat_b, m, second)
    halo_start(1)
    for m in range(MICROS):
        second = cat_b[m, 1 : 1 + ROWS, :, CH : 2 * CH].reshape(HALF, CH).astype(F32)
        x2t[:, tokens_of(m)] = second.T.astype(BF)
    halo_wait(1, cat_b)
    for m in range(MICROS):
        update = conv(cat_b, 1, m)
        out[tokens_of(m), :] = (section_in[tokens_of(m), :].astype(F32) + update).astype(BF)

    def sum_copy(k, device):
        return pltpu.make_async_remote_copy(
            src_ref=hsum.at[k],
            dst_ref=hgot.at[k],
            send_sem=sum_s.at[k],
            recv_sem=sum_r.at[k],
            device_id=device,
            device_id_type=MESH,
        )

    rounds = [y1, dp_peer, z1, z2, x1, x2]

    def sum_start(k):
        @pl.when(seg == 1)
        def _():
            sum_copy(k, rounds[k]).start()

    def sum_end(k):
        @pl.when(seg == 1)
        def _():
            sum_copy(k, rounds[k]).wait()
            hsum[k + 1] = hsum[k] + hgot[k]

    @pl.when(seg == 0)
    def _():
        to_next = seg_copy(out, inc, 0)
        to_next.start()
        to_next.wait_send()
        seg_copy(grad_ref, og_in, 1).wait_recv()
        og[...] = og_in[...]

    @pl.when(seg == 1)
    def _():
        hw = head_pad[...].astype(BF)
        o = out[...]
        logits = dot(hw, o, ((1,), (1,)))
        albedo = 1.0 / (1.0 + jnp.exp(-logits))
        row = lax.broadcasted_iota(jnp.int32, (8, TOKENS), 0)
        lane = lax.broadcasted_iota(jnp.int32, (8, TOKENS), 1)
        tint = jnp.zeros((8, TOKENS), F32)
        for m in range(MICROS):
            light = illum_ref[m, x]
            for c in range(3):
                tint = jnp.where((row == c) & (lane // HALF == m), light_ref[light, c], tint)
        mismatch = albedo * tint - targets[...]
        squares = jnp.sum(mismatch * mismatch)
        lg = (factor * mismatch * tint * albedo * (1.0 - albedo)).astype(BF)
        hg = dot(lg, o)
        row_h = lax.broadcasted_iota(jnp.int32, (8, CH), 0)
        hsum[0] = jnp.where(row_h == 3, squares, hg)
        lgt = lg.astype(F32).T.astype(BF)
        og[...] = dot(lgt, hw).astype(BF)

    sum_start(0)

    for m in range(MICROS):
        g = og[tokens_of(m), :].astype(F32)
        edges(2, m, g)
        fill(cat_c, m, g)
    halo_start(2)
    halo_wait(2, cat_c)
    sum_end(0)
    sum_start(1)
    for m in range(MICROS):
        sg = conv_back(cat_c, 1, m)
        hg = (sg * gelu_slope(hidden[tokens_of(m), :])).astype(BF).astype(F32)
        edges(3, m, hg)
        fill(cat_a, m, hg)
    halo_start(3)
    sum_end(1)
    sum_start(2)
    conv_weight_grad(x2t, cat_c, 1)
    halo_wait(3, cat_a)
    sum_end(2)
    sum_start(3)
    for m in range(MICROS):
        fg = conv_back(cat_a, 0, m)
        rows = tokens_of(m)
        slope = gelu_slope(section_in[rows, :].astype(F32))
        grad_ref[rows, :] = (og[rows, :].astype(F32) + fg * slope).astype(BF)

    @pl.when(seg == 1)
    def _():
        seg_copy(grad_ref, og_in, 1).start()

    sum_end(3)
    sum_start(4)
    conv_weight_grad(x1t, cat_a, 0)
    sum_end(4)
    sum_start(5)
    sum_end(5)

    final = pltpu.make_async_remote_copy(
        src_ref=hsum.at[6],
        dst_ref=hfin,
        send_sem=seg_s.at[2],
        recv_sem=seg_r.at[2],
        device_id=sibling,
        device_id_type=MESH,
    )

    @pl.when(seg == 1)
    def _():
        final.start()
        total_ref[...] = hsum[6]
        seg_copy(grad_ref, og_in, 1).wait_send()
        final.wait_send()

    @pl.when(seg == 0)
    def _():
        final.wait_recv()
        total_ref[...] = hfin[...]


class Reduce:
    def __init__(self, axis, own, store, stage, got, send, recv):
        self.a = axis
        self.own, self.store = own, store
        self.stage, self.got, self.send, self.recv = stage, got, send, recv
        self.copies = []

    def put(self, k, value, device):
        self.stage[k] = value.astype(BF)
        copy = pltpu.make_async_remote_copy(
            src_ref=self.stage.at[k],
            dst_ref=self.got.at[k],
            send_sem=self.send.at[k],
            recv_sem=self.recv.at[k],
            device_id=device,
            device_id_type=MESH,
        )
        copy.start()
        self.copies.append(copy)

    def take(self, k):
        pltpu.make_async_remote_copy(
            src_ref=self.stage.at[k],
            dst_ref=self.got.at[k],
            send_sem=self.send.at[k],
            recv_sem=self.recv.at[k],
            device_id=self.a.device(0, 1, 0),
            device_id_type=MESH,
        ).wait_recv()
        return self.got[k].astype(F32)

    def part(self, dp, r, dq):
        return self.own(self.a.slot(dp, r, dq))

    def first(self, i):
        dp, r = BACK[i]
        way = -1 if r == 0 else 1
        self.put(i, self.part(dp, r, 2), self.a.device(0, 0, way))
        self.put(16 + i, self.part(dp, r, -way), self.a.device(0, 0, -way))

    def second(self, i):
        dp, r = BACK[i]
        way = -1 if r == 0 else 1
        self.put(8 + i, self.part(dp, r, way) + self.take(i), self.a.device(0, 0, way))

    def third(self, i):
        dp, r = BACK[i]
        way = -1 if r == 0 else 1
        total = self.part(dp, r, 0) + self.take(8 + i) + self.take(16 + i)
        if dp == 2:
            self.put(24 + r, total, self.a.device(way, 0, 0))
        elif dp == way:
            self.put(26 + r, total + self.take(24 + r), self.a.device(way, 0, 0))
        elif dp == -way:
            self.put(28 + r, total, self.a.device(-way, 0, 0))
        else:
            total = total + self.take(26 + r) + self.take(28 + r)
            if r == 1:
                self.put(30, total, self.a.device(0, 1, 0))
            else:
                self.kept = total

    def fourth(self):
        self.kept = self.kept + self.take(30)
        self.put(31, self.kept, {"dp": 1 - lax.axis_index("dp")})

    def fifth(self):
        self.store(self.stage[31].astype(F32) + self.take(31))
        for copy in self.copies:
            copy.wait_send()


def reduce_kernel(
    hooks_ref,
    grad_ref,
    gconv_ref,
    proj_out,
    conv_out,
    hooks_v,
    part,
    pstage,
    pgot,
    cstage,
    cgot,
    load_sem,
    ps,
    pr,
    cs,
    cr,
):
    x, y, z = place()
    pa = Axis(True)
    loads = []
    for i, (dp, r) in enumerate(BACK):
        xs, ys, _ = pa.coords(dp, r, 0)
        start = pl.multiple_of((xs * 2 + ys) * CHUNK, CHUNK)
        copy = pltpu.make_async_copy(
            hooks_ref.at[:, pl.ds(start, CHUNK)], hooks_v.at[i], load_sem.at[i]
        )
        copy.start()
        loads.append(copy)
    entry_barrier(
        [
            at((x + 1) % 4, y, z),
            at((x + 3) % 4, y, z),
            at(x, y, (z + 1) % 4),
            at(x, y, (z + 3) % 4),
            at(x, 1 - y, z),
            {"dp": 1 - lax.axis_index("dp")},
        ]
    )

    def own_conv(slot):
        start = pl.multiple_of(slot * CSLOT, 8)
        return gconv_ref[:, pl.ds(start, CSLOT), :]

    def own_proj(slot):
        return part[slot]

    def store_conv(v):
        conv_out[...] = v

    def store_proj(v):
        proj_out[...] = v

    rc = Reduce(Axis(False), own_conv, store_conv, cstage, cgot, cs, cr)
    rp = Reduce(pa, own_proj, store_proj, pstage, pgot, ps, pr)

    def compute(i):
        loads[i].wait()
        dp, r = BACK[i]
        xs, ys, _ = pa.coords(dp, r, 0)
        base = xs * 8 + ys * 4
        v = dot(hooks_v[i], grad_ref[...], ((0,), (0,)))
        for k in range(4):
            part[base + k] = v[k * SLOT : (k + 1) * SLOT]

    rc.first(0)
    rc.first(1)
    for i in range(8):
        compute(i)
        rp.first(i)
        if i + 2 < 8:
            rc.first(i + 2)
        if i >= 1:
            rc.second(i - 1)
        if i >= 2:
            rp.second(i - 2)
    rc.second(7)
    rp.second(6)
    rp.second(7)
    for i in range(8):
        rc.third(i)
        rp.third(i)
    rc.fourth()
    rp.fourth()
    rc.fifth()
    rp.fifth()


def run_main(npix, factor, hooks, proj, conv, head, light, illum, offsets, photos):
    vm = pl.BlockSpec(memory_space=pltpu.VMEM)
    sm = pl.BlockSpec(memory_space=pltpu.SMEM)
    dma = pltpu.SemaphoreType.DMA
    return pl.pallas_call(
        functools.partial(main_kernel, npix, factor),
        out_shape=(
            jax.ShapeDtypeStruct((TOKENS, CH), BF),
            jax.ShapeDtypeStruct((2, 9 * CH, CH), F32),
            jax.ShapeDtypeStruct((8, CH), F32),
        ),
        in_specs=[pl.BlockSpec(memory_space=pl.ANY), vm, vm, vm, sm, sm, sm, vm],
        out_specs=(vm, vm, vm),
        scratch_shapes=[
            pltpu.VMEM((8, TOKENS, CHUNK), BF),
            pltpu.VMEM((32, SLOT, CH), BF),
            pltpu.VMEM((32, 2, CSLOT, CH), BF),
            pltpu.VMEM((2, 9 * CH, CH), F32),
            pltpu.VMEM((2, 9 * CH, CH), BF),
            pltpu.VMEM((TOKENS, CH), F32),
            pltpu.VMEM((TOKENS, CH), BF),
            pltpu.VMEM((TOKENS, CH), BF),
            pltpu.VMEM((TOKENS, CH), BF),
            pltpu.VMEM((TOKENS, CH), BF),
            pltpu.VMEM((TOKENS, CH), BF),
            pltpu.VMEM((TOKENS, CH), F32),
            pltpu.VMEM((MICROS, ROWS + 2, COLS, 3 * CH), BF),
            pltpu.VMEM((MICROS, ROWS + 2, COLS, 3 * CH), BF),
            pltpu.VMEM((MICROS, ROWS + 2, COLS, 3 * CH), BF),
            pltpu.VMEM((CH, TOKENS), BF),
            pltpu.VMEM((CH, TOKENS), BF),
            pltpu.VMEM((4, 2, MICROS, COLS, CH), BF),
            pltpu.VMEM((4, 2, MICROS, COLS, CH), BF),
            pltpu.VMEM((8, TOKENS), F32),
            pltpu.VMEM((8, CH), F32),
            pltpu.VMEM((7, 8, CH), F32),
            pltpu.VMEM((6, 8, CH), F32),
            pltpu.VMEM((8, CH), F32),
            dma((8,)),
            dma((32,)),
            dma((32,)),
            dma((32,)),
            dma((32,)),
            dma((4, 2)),
            dma((4, 2)),
            dma((3,)),
            dma((3,)),
            dma((6,)),
            dma((6,)),
        ],
        compiler_params=pltpu.CompilerParams(
            collective_id=0, has_side_effects=True, vmem_limit_bytes=56 * 1024 * 1024
        ),
        cost_estimate=pl.CostEstimate(
            flops=11_000_000_000, bytes_accessed=20_000_000, transcendentals=1_000_000
        ),
        name="main_kernel",
    )(hooks, proj, conv, head, light, illum, offsets, photos)


def run_reduce(hooks, grad, gconv):
    vm = pl.BlockSpec(memory_space=pltpu.VMEM)
    dma = pltpu.SemaphoreType.DMA
    return pl.pallas_call(
        reduce_kernel,
        out_shape=(
            jax.ShapeDtypeStruct((SLOT, CH), F32),
            jax.ShapeDtypeStruct((2, CSLOT, CH), F32),
        ),
        in_specs=[pl.BlockSpec(memory_space=pl.ANY), vm, vm],
        out_specs=(vm, vm),
        scratch_shapes=[
            pltpu.VMEM((8, TOKENS, CHUNK), BF),
            pltpu.VMEM((32, SLOT, CH), F32),
            pltpu.VMEM((32, SLOT, CH), BF),
            pltpu.VMEM((32, SLOT, CH), BF),
            pltpu.VMEM((32, 2, CSLOT, CH), BF),
            pltpu.VMEM((32, 2, CSLOT, CH), BF),
            dma((8,)),
            dma((32,)),
            dma((32,)),
            dma((32,)),
            dma((32,)),
        ],
        compiler_params=pltpu.CompilerParams(
            collective_id=1, has_side_effects=True, vmem_limit_bytes=56 * 1024 * 1024
        ),
        cost_estimate=pl.CostEstimate(
            flops=3_300_000_000, bytes_accessed=20_000_000, transcendentals=0
        ),
        name="reduce_kernel",
    )(hooks, grad, gconv)


def body(hooks, proj_weight, conv_weight, head_weight, light_color, illum, offsets, photos):
    npix = 3 * MICROS * lax.axis_size("dp") * ROWS * lax.axis_size("fsdp") * COLS
    factor = 2.0 * LOSS_SCALE / npix
    tokens = hooks.reshape(TOKENS, D)
    grad, gconv, total = run_main(
        npix, factor, tokens, proj_weight[0], conv_weight[0], head_weight, light_color,
        illum, offsets, photos,
    )
    grad_proj, grad_conv = run_reduce(tokens, grad, gconv)
    return (grad_proj[None], grad_conv[None], total[:3], total[3, 0] / npix)


def solution(mesh):
    placed = (
        P("segment", "dp", "fsdp", None, None),
        P("segment", "fsdp", None),
        P("segment", None, "fsdp", None),
        P(),
        P(),
        P("dp", None),
        P("dp", None, None),
        P("dp", None, None, None, None),
    )
    return jax.shard_map(
        body,
        mesh=mesh,
        in_specs=placed,
        out_specs=(P("segment", "fsdp", None), P("segment", None, "fsdp", None), P(), P()),
        check_vma=False,
    )
```

```python
import functools

import jax
import jax.numpy as jnp
from jax import lax
from jax.experimental import pallas as pl
from jax.experimental.pallas import tpu as pltpu
from jax.sharding import PartitionSpec as P

LOSS_SCALE = 8192.0
MESH = pl.DeviceIdType.MESH
BF = jnp.bfloat16
F32 = jnp.float32

MICROS, ROWS, COLS, CH = 2, 8, 64, 256
TOKENS = MICROS * ROWS * COLS
HALF = ROWS * COLS
D = 6144
SLOT = 192
CSLOT = 72
CHUNK = 4 * SLOT

ORDER = [(0, 0), (1, 0), (-1, 0), (0, 1), (2, 0), (1, 1), (-1, 1), (2, 1)]
PLANE = ORDER[1:]
BACK = ORDER[::-1]


def place():
    f = lax.axis_index("fsdp")
    return f // 8, (f // 4) % 2, f % 4


def at(x, y, z):
    return {"fsdp": x * 8 + y * 4 + z}


def dot(a, b, dims=((1,), (0,))):
    return lax.dot_general(a, b, (dims, ((), ())), preferred_element_type=F32)


def gelu_parts(v):
    c = 0.7978845608028654
    t = jnp.tanh(c * (v + 0.044715 * (v * v * v)))
    return t


def gelu(v):
    return 0.5 * v * (1.0 + gelu_parts(v))


def gelu_slope(v):
    c = 0.7978845608028654
    t = gelu_parts(v)
    return 0.5 * (1.0 + t) + 0.5 * v * (1.0 - t * t) * (c * (1.0 + 3.0 * 0.044715 * (v * v)))


class Axis:
    def __init__(self, p_is_x):
        x, y, z = place()
        self.p_is_x = p_is_x
        self.p, self.y, self.q = (x, y, z) if p_is_x else (z, y, x)

    def coords(self, dp, r, dq):
        p = (self.p + (dp + 4)) % 4
        q = (self.q + (dq + 4)) % 4
        y = (self.y + r) % 2
        return (p, y, q) if self.p_is_x else (q, y, p)

    def slot(self, dp, r, dq):
        x, y, z = self.coords(dp, r, dq)
        return x * 8 + y * 4 + z

    def device(self, dp, r, dq):
        return at(*self.coords(dp, r, dq))


def rel(dp, r, dq):
    return ((dp % 4) * 2 + r) * 4 + dq % 4


class Gather:
    def __init__(self, axis, buf, send, recv):
        self.a, self.buf, self.send, self.recv = axis, buf, send, recv
        self.copies = []

    def put(self, dp, r, dq, to):
        tp, tr, tq = to
        a = self.a
        slot = a.slot(dp, r, dq)
        copy = pltpu.make_async_remote_copy(
            src_ref=self.buf.at[slot],
            dst_ref=self.buf.at[slot],
            send_sem=self.send.at[len(self.copies)],
            recv_sem=self.recv.at[rel(dp - tp, (r + tr) % 2, dq - tq)],
            device_id=a.device(tp, tr, tq),
            device_id_type=MESH,
        )
        copy.start()
        self.copies.append(copy)

    def await_(self, dp, r, dq):
        a = self.a
        slot = a.slot(dp, r, dq)
        pltpu.make_async_remote_copy(
            src_ref=self.buf.at[slot],
            dst_ref=self.buf.at[slot],
            send_sem=self.send.at[0],
            recv_sem=self.recv.at[rel(dp, r, dq)],
            device_id=a.device(0, 1, 0),
            device_id_type=MESH,
        ).wait_recv()

    def spread(self):
        for dp, r in PLANE:
            self.put(0, 0, 0, (dp, r, 0))

    def along(self, i):
        dp, r = ORDER[i]
        if i > 0:
            self.await_(dp, r, 0)
        for dq in (1, -1, 2):
            self.put(dp, r, 0, (0, 0, dq))

    def last(self, i):
        dp, r = ORDER[i]
        for dq in (1, -1, 2):
            self.await_(dp, r, dq)

    def drain(self):
        for copy in self.copies:
            copy.wait_send()


def entry_barrier(devices):
    barrier = pltpu.get_barrier_semaphore()
    for device in devices:
        pl.semaphore_signal(barrier, inc=1, device_id=device, device_id_type=MESH)
    pl.semaphore_wait(barrier, len(devices))


def partners():
    pa, pc = Axis(True), Axis(False)
    return [pa.device(dp, r, 0) for dp, r in PLANE] + [
        pc.device(dp, r, 0) for dp, r in PLANE if dp != 0
    ]


def load_rows(source, target, sem):
    copies = []
    for i in range(8):
        rows = pl.ds(i * (TOKENS // 8), TOKENS // 8)
        copy = pltpu.make_async_copy(source.at[rows, :], target.at[rows, :], sem.at[i])
        copy.start()
        copies.append(copy)
    return copies


def shift_parts(v):
    n = v.shape[0]
    col = lax.broadcasted_iota(jnp.int32, v.shape, 0) % COLS
    before = jnp.where(col == 0, 0.0, pltpu.roll(v, 1, 0))
    after = jnp.where(col == COLS - 1, 0.0, pltpu.roll(v, n - 1, 0))
    return before.astype(BF), v.astype(BF), after.astype(BF)


class Reduce:
    def __init__(self, axis, own, store, stage, got, send, recv, placed=False):
        self.a = axis
        self.own, self.store = own, store
        self.stage, self.got, self.send, self.recv = stage, got, send, recv
        self.placed = placed
        self.copies = []

    def put(self, k, value, device):
        if value is not None:
            self.stage[k] = value.astype(BF)
        copy = pltpu.make_async_remote_copy(
            src_ref=self.stage.at[k],
            dst_ref=self.got.at[k],
            send_sem=self.send.at[k],
            recv_sem=self.recv.at[k],
            device_id=device,
            device_id_type=MESH,
        )
        copy.start()
        self.copies.append(copy)

    def take(self, k):
        pltpu.make_async_remote_copy(
            src_ref=self.stage.at[k],
            dst_ref=self.got.at[k],
            send_sem=self.send.at[k],
            recv_sem=self.recv.at[k],
            device_id=self.a.device(0, 1, 0),
            device_id_type=MESH,
        ).wait_recv()
        return self.got[k].astype(F32)

    def part(self, dp, r, dq, i):
        return self.own(self.a.slot(dp, r, dq), dq, i)

    def first(self, i):
        dp, r = BACK[i]
        for j, dq in enumerate((2, 1, -1)):
            value = None if self.placed else self.part(dp, r, dq, i)
            self.put(3 * i + j, value, self.a.device(0, 0, dq))

    def second(self, i):
        dp, r = BACK[i]
        total = self.part(dp, r, 0, i)
        for j in range(3):
            total = total + self.take(3 * i + j)
        if i < 7:
            self.put(24 + i, total, self.a.device(dp, r, 0))
        else:
            self.kept = total

    def third(self):
        for i in range(7):
            self.kept = self.kept + self.take(24 + i)
        self.put(31, self.kept, {"dp": 1 - lax.axis_index("dp")})

    def fourth(self):
        self.store(self.stage[31].astype(F32) + self.take(31))
        for copy in self.copies:
            copy.wait_send()


def main_kernel(
    factor,
    hooks_ref,
    proj_ref,
    conv_ref,
    head_ref,
    light_ref,
    illum_ref,
    offsets_ref,
    photos_ref,
    proj_out,
    conv_out,
    total_ref,
    hooks_v,
    wproj,
    wconv,
    wf32,
    wbf,
    wflip,
    acc,
    section_in,
    inc,
    out,
    og_in,
    og,
    grad,
    hidden,
    cat_a,
    cat_b,
    cat_c,
    cat_d,
    x1t,
    x2t,
    hsend,
    hrecv,
    targets,
    head_pad,
    hsum,
    hgot,
    hfin,
    part,
    pgot,
    cgot,
    load_sem,
    psend,
    precv,
    csend,
    crecv,
    hs_sem,
    hr_sem,
    seg_s,
    seg_r,
    sum_s,
    sum_r,
    rps,
    rpr,
    rcs,
    rcr,
    gate,
):
    x, y, z = place()
    seg = lax.axis_index("segment")
    dpi = lax.axis_index("dp")
    band = y * 4 + z
    sibling = {"segment": 1 - seg}
    dp_peer = {"dp": 1 - dpi}
    up_j, down_j = (band + 7) % 8, (band + 1) % 8
    up = at(x, up_j // 4, up_j % 4)
    down = at(x, down_j // 4, down_j % 4)
    up_other = {"segment": 1 - seg, **up}
    down_other = {"segment": 1 - seg, **down}

    pa = Axis(True)
    loads = load_rows(hooks_ref, hooks_v, load_sem)

    me = x * 8 + y * 4 + z
    wproj[me] = proj_ref[...]
    wconv[me] = conv_ref[...]

    z1 = at(x, y, z + 1 - 2 * (z % 2))
    z2 = at(x, y, (z + 2) % 4)
    x1 = at(x + 1 - 2 * (x % 2), y, z)
    x2 = at((x + 2) % 4, y, z)
    y1 = at(x, 1 - y, z)
    entry_barrier(partners() + [sibling, dp_peer, up_other, down_other])

    gp = Gather(pa, wproj, psend, precv)
    gc = Gather(Axis(False), wconv, csend, crecv)

    @pl.when(seg == 1)
    def _():
        pl.semaphore_wait(gate, 1)

    gp.spread()
    gc.spread()
    gp.along(0)
    gc.along(0)

    yy = lax.broadcasted_iota(jnp.int32, (96, HALF), 0)
    nn = lax.broadcasted_iota(jnp.int32, (96, HALF), 1)
    row8 = lax.broadcasted_iota(jnp.int32, (8, HALF), 0)
    for m in range(MICROS):
        oy = offsets_ref[m, 0, x]
        ox = offsets_ref[m, 1, x]
        pick_col = (yy == ox + nn % COLS).astype(F32).astype(BF)
        pick_row = yy == oy + band * ROWS + nn // COLS
        block = jnp.zeros((8, HALF), F32)
        for c in range(3):
            q = dot(photos_ref[m, x, c], pick_col)
            line = jnp.sum(jnp.where(pick_row, q, 0.0), axis=0, keepdims=True)
            block = jnp.where(row8 == c, line, block)
        targets[:, m * HALF : (m + 1) * HALF] = block
    head_pad[...] = jnp.zeros((8, CH), F32)
    head_pad[0:3, :] = head_ref[...].astype(F32)

    acc[...] = jnp.zeros_like(acc)
    for copy in loads:
        copy.wait()

    def project(i):
        dp, r = ORDER[i]
        xs, ys, _ = pa.coords(dp, r, 0)
        base = xs * 8 + ys * 4
        lanes = pl.ds(pl.multiple_of(base * SLOT, CHUNK), CHUNK)
        w = wproj[pl.ds(base, 4)].reshape(CHUNK, CH)

        def step(t, _):
            rows = pl.ds(pl.multiple_of(t * 256, 256), 256)
            acc[rows, :] += dot(hooks_v[rows, lanes], w)
            return 0

        lax.fori_loop(0, TOKENS // 256, step, 0)

    for i in range(1, 8):
        gp.along(i)
        gc.along(i)
        if i == 7:

            @pl.when(seg == 0)
            def _():
                pl.semaphore_signal(gate, inc=1, device_id=sibling, device_id_type=MESH)

        if i >= 2:
            gp.last(i - 2)
            gc.last(i - 2)
            project(i - 2)
    gc.last(6)
    gc.last(7)

    def gather_rows(k, _):
        start = pl.multiple_of(k * CSLOT, 8)
        wf32[0, pl.ds(start, CSLOT), :] = wconv[k, 0].astype(F32)
        wf32[1, pl.ds(start, CSLOT), :] = wconv[k, 1].astype(F32)
        return 0

    lax.fori_loop(0, 32, gather_rows, 0)

    def to_bf(k, _):
        start = pl.multiple_of(k * CH, CH)
        wbf[0, pl.ds(start, CH), :] = wf32[0, pl.ds(start, CH), :].astype(BF)
        wbf[1, pl.ds(start, CH), :] = wf32[1, pl.ds(start, CH), :].astype(BF)
        return 0

    lax.fori_loop(0, 9, to_bf, 0)
    gp.last(6)
    project(6)
    gp.last(7)
    project(7)

    def flip_weights():
        def step(k, _):
            source = pl.ds(pl.multiple_of(k * CH, CH), CH)
            target = pl.ds(pl.multiple_of((8 - k) * CH, CH), CH)
            wflip[0, target, :] = wf32[0, source, :].T.astype(BF)
            wflip[1, target, :] = wf32[1, source, :].T.astype(BF)
            return 0

        lax.fori_loop(0, 9, step, 0)

    def seg_copy(src, dst, k):
        return pltpu.make_async_remote_copy(
            src_ref=src,
            dst_ref=dst,
            send_sem=seg_s.at[k],
            recv_sem=seg_r.at[k],
            device_id=sibling,
            device_id_type=MESH,
        )

    def halo(e, side, device):
        return pltpu.make_async_remote_copy(
            src_ref=hsend.at[e, side],
            dst_ref=hrecv.at[e, 1 - side],
            send_sem=hs_sem.at[e, side],
            recv_sem=hr_sem.at[e, 1 - side],
            device_id=device,
            device_id_type=MESH,
        )

    def halo_start(e, to_up, to_down):
        halo(e, 0, to_up).start()
        halo(e, 1, to_down).start()

    def halo_sent(e):
        halo(e, 0, up).wait_send()
        halo(e, 1, up).wait_send()

    def halo_here(e):
        halo(e, 0, up).wait_recv()
        halo(e, 1, up).wait_recv()

    def edges(e, source):
        for m in range(MICROS):
            hsend[e, 0, m] = source[m * HALF : m * HALF + 2 * COLS, :]
            hsend[e, 1, m] = source[(m + 1) * HALF - 2 * COLS : (m + 1) * HALF, :]

    def fill(cat, m, row, value):
        a, b, c = shift_parts(value)
        n = value.shape[0] // COLS
        cat[m, row : row + n, :, 0:CH] = a.reshape(n, COLS, CH)
        cat[m, row : row + n, :, CH : 2 * CH] = b.reshape(n, COLS, CH)
        cat[m, row : row + n, :, 2 * CH : 3 * CH] = c.reshape(n, COLS, CH)

    def tokens_of(m):
        return slice(m * HALF, (m + 1) * HALF)

    def conv(weights, which, left):
        total = None
        for ky in range(3):
            value = left(ky)
            value = value.reshape(-1, 3 * CH)
            piece = dot(value, weights[which, ky * 3 * CH : (ky + 1) * 3 * CH, :])
            total = piece if total is None else total + piece
        return total

    def conv_weight_grad(xt, cat, low, which):
        for ky in range(3):
            total = None
            for m in range(MICROS):
                right = cat[m, low - ky : low - ky + ROWS].reshape(HALF, 3 * CH)
                piece = dot(xt[:, tokens_of(m)], right)
                total = piece if total is None else total + piece
            for kx in range(3):
                j = 2 - kx
                row = (3 * ky + kx) * CH
                wf32[which, row : row + CH, :] = total[:, j * CH : (j + 1) * CH]

    def two_convs(cat, weights, first, middle, mid, second, halo_ready):
        for m in range(MICROS):
            v = conv(weights, first, lambda ky: cat[m, 2 + ky : 8 + ky])
            fill(mid, m, 2, middle(m, 1, 6, v))
        halo_ready()
        for low, edge in ((0, 0), (8, 7)):
            v = conv(weights, first, lambda ky: cat[:, low + ky : low + ky + 2])
            for m in range(MICROS):
                u = middle(m, low - 1, 2, v[m * 2 * COLS : (m + 1) * 2 * COLS])
                outer = lax.broadcasted_iota(jnp.int32, u.shape, 0) // COLS == edge // 7
                u = jnp.where(jnp.logical_and(outer, band == edge), 0.0, u)
                fill(mid, m, low, u)
        return [conv(weights, second, lambda ky, m=m: mid[m, ky : ky + ROWS]) for m in range(MICROS)]

    def halo_rows(cat, rows_of):
        for side, row, last in ((0, 0, 0), (1, ROWS + 2, 7)):
            for m in range(MICROS):
                v = rows_of(side, m)
                v = jnp.where(band == last, jnp.zeros_like(v), v)
                fill(cat, m, row, v)

    section_in[...] = acc[...].astype(BF)
    edges(0, section_in)
    halo_start(0, up, down)
    gp.drain()
    gc.drain()

    @pl.when(seg == 1)
    def _():
        flip_weights()
        seg_copy(out, inc, 0).wait_recv()
        section_in[...] = (section_in[...].astype(F32) + inc[...].astype(F32)).astype(BF)

    for m in range(MICROS):
        fill(cat_a, m, 2, gelu(section_in[tokens_of(m), :].astype(F32)).astype(BF).astype(F32))

    def forward_halo():
        halo_here(0)

        @pl.when(seg == 1)
        def _():
            halo_here(1)

        def rows_of(side, m):
            shape = (2 * COLS, CH)
            more = jnp.where(seg == 1, hrecv[1, side, m].astype(F32), 0.0)
            v = (hrecv[0, side, m].astype(F32) + more).astype(BF).astype(F32)
            return gelu(v).astype(BF).astype(F32)

        halo_rows(cat_a, rows_of)

    def keep_hidden(m, row, n, v):
        hidden[m, row + 1 : row + 1 + n] = v.reshape(n, COLS, CH)
        return gelu(v).astype(BF).astype(F32)

    update = two_convs(cat_a, wbf, 0, keep_hidden, cat_b, 1, forward_halo)
    for m in range(MICROS):
        out[tokens_of(m), :] = (section_in[tokens_of(m), :].astype(F32) + update[m]).astype(BF)

    def transposes():
        for m in range(MICROS):
            v = cat_a[m, 2 : 2 + ROWS, :, CH : 2 * CH].reshape(HALF, CH).astype(F32)
            x1t[:, tokens_of(m)] = v.T.astype(BF)
            v = cat_b[m, 1 : 1 + ROWS, :, CH : 2 * CH].reshape(HALF, CH).astype(F32)
            x2t[:, tokens_of(m)] = v.T.astype(BF)

    def sum_copy(k, device):
        return pltpu.make_async_remote_copy(
            src_ref=hsum.at[k],
            dst_ref=hgot.at[k],
            send_sem=sum_s.at[k],
            recv_sem=sum_r.at[k],
            device_id=device,
            device_id_type=MESH,
        )

    rounds = [y1, dp_peer, z1, z2, x1, x2]

    def sum_start(k):
        @pl.when(seg == 1)
        def _():
            sum_copy(k, rounds[k]).start()

    def sum_end(k):
        @pl.when(seg == 1)
        def _():
            sum_copy(k, rounds[k]).wait()
            hsum[k + 1] = hsum[k] + hgot[k]

    @pl.when(seg == 0)
    def _():
        edges(1, out)
        halo_start(1, up_other, down_other)
        to_next = seg_copy(out, inc, 0)
        to_next.start()
        flip_weights()
        transposes()
        to_next.wait_send()
        halo_sent(1)
        seg_copy(grad, og_in, 1).wait_recv()
        og[...] = og_in[...]

    @pl.when(seg == 1)
    def _():
        hw = head_pad[...].astype(BF)
        o = out[...]
        logits = dot(hw, o, ((1,), (1,)))
        albedo = 1.0 / (1.0 + jnp.exp(-logits))
        row = lax.broadcasted_iota(jnp.int32, (8, TOKENS), 0)
        lane = lax.broadcasted_iota(jnp.int32, (8, TOKENS), 1)
        tint = jnp.zeros((8, TOKENS), F32)
        for m in range(MICROS):
            light = illum_ref[m, x]
            for c in range(3):
                tint = jnp.where((row == c) & (lane // HALF == m), light_ref[c, light], tint)
        mismatch = albedo * tint - targets[...]
        lg = (factor * mismatch * tint * albedo * (1.0 - albedo)).astype(BF)
        lgt = lg.astype(F32).T.astype(BF)
        og[...] = dot(lgt, hw).astype(BF)
        edges(2, og)
        halo_start(2, up, down)
        squares = jnp.sum(mismatch * mismatch)
        hg = dot(lg, o)
        row_h = lax.broadcasted_iota(jnp.int32, (8, CH), 0)
        hsum[0] = jnp.where(row_h == 3, squares, hg)

    sum_start(0)

    for m in range(MICROS):
        fill(cat_c, m, 2, og[tokens_of(m), :].astype(F32))

    def backward_halo():
        @pl.when(seg == 1)
        def _():
            halo_here(2)

        @pl.when(seg == 0)
        def _():
            halo_here(3)

        def rows_of(side, m):
            v = jnp.where(seg == 1, hrecv[2, side, m].astype(F32), hrecv[3, side, m].astype(F32))
            return v

        halo_rows(cat_c, rows_of)

    def through(m, row, n, v):
        h = hidden[m, row + 1 : row + 1 + n].reshape(n * COLS, CH)
        return (v * gelu_slope(h)).astype(BF).astype(F32)

    back = two_convs(cat_c, wflip, 1, through, cat_d, 0, backward_halo)
    for m in range(MICROS):
        rows = tokens_of(m)
        slope = gelu_slope(section_in[rows, :].astype(F32))
        grad[rows, :] = (og[rows, :].astype(F32) + back[m] * slope).astype(BF)

    @pl.when(seg == 1)
    def _():
        edges(3, grad)
        halo_start(3, up_other, down_other)
        seg_copy(grad, og_in, 1).start()
        transposes()

    sum_end(0)
    sum_start(1)
    conv_weight_grad(x2t, cat_c, 3, 1)
    sum_end(1)
    sum_start(2)
    conv_weight_grad(x1t, cat_d, 2, 0)
    sum_end(2)
    sum_start(3)

    def own_conv(slot, dq, i):
        start = pl.multiple_of(slot * CSLOT, 8)
        return wf32[:, pl.ds(start, CSLOT), :]

    def own_proj(slot, dq, i):
        return part[i]

    def store_conv(v):
        conv_out[...] = v

    def store_proj(v):
        proj_out[...] = v

    rc = Reduce(Axis(False), own_conv, store_conv, wconv, cgot, rcs, rcr)
    rp = Reduce(pa, own_proj, store_proj, wproj, pgot, rps, rpr, placed=True)

    def compute(i):
        dp, r = BACK[i]
        xs, ys, _ = pa.coords(dp, r, 0)
        base = xs * 8 + ys * 4
        lanes = pl.ds(pl.multiple_of(base * SLOT, CHUNK), CHUNK)
        v = dot(hooks_v[:, lanes], grad[...], ((0,), (0,)))
        for k in range(4):
            ahead = (k - z + 4) % 4
            block = v[k * SLOT : (k + 1) * SLOT]
            for dq, j in ((0, None), (2, 0), (1, 1), (3, 2)):

                @pl.when(ahead == dq)
                def _():
                    if j is None:
                        part[i] = block
                    else:
                        wproj[3 * i + j] = block.astype(BF)

        rp.first(i)

    for i in range(8):
        rc.first(i)
        compute(i)
        if i in (1, 3, 5):
            sum_end(3 + i // 2)
            if i < 5:
                sum_start(4 + i // 2)
        if i >= 2:
            rc.second(i - 2)
            rp.second(i - 2)
    final = pltpu.make_async_remote_copy(
        src_ref=hsum.at[6],
        dst_ref=hfin,
        send_sem=seg_s.at[2],
        recv_sem=seg_r.at[2],
        device_id=sibling,
        device_id_type=MESH,
    )

    @pl.when(seg == 1)
    def _():
        final.start()
        total_ref[...] = hsum[6]

    for i in (6, 7):
        rc.second(i)
        rp.second(i)
    rc.third()
    rp.third()
    rc.fourth()
    rp.fourth()
    halo_sent(0)

    @pl.when(seg == 1)
    def _():
        halo_sent(2)
        halo_sent(3)
        seg_copy(grad, og_in, 1).wait_send()
        final.wait_send()

    @pl.when(seg == 0)
    def _():
        final.wait_recv()
        total_ref[...] = hfin[...]


def run_main(factor, hooks, proj, conv, head, light, illum, offsets, photos):
    vm = pl.BlockSpec(memory_space=pltpu.VMEM)
    sm = pl.BlockSpec(memory_space=pltpu.SMEM)
    dma = pltpu.SemaphoreType.DMA
    field = pltpu.VMEM((TOKENS, CH), BF)
    return pl.pallas_call(
        functools.partial(main_kernel, factor),
        out_shape=(
            jax.ShapeDtypeStruct((SLOT, CH), F32),
            jax.ShapeDtypeStruct((2, CSLOT, CH), F32),
            jax.ShapeDtypeStruct((8, CH), F32),
        ),
        in_specs=[pl.BlockSpec(memory_space=pl.ANY), vm, vm, vm, sm, sm, sm, vm],
        out_specs=(vm, vm, vm),
        scratch_shapes=[
            pltpu.VMEM((TOKENS, D), BF),
            pltpu.VMEM((32, SLOT, CH), BF),
            pltpu.VMEM((32, 2, CSLOT, CH), BF),
            pltpu.VMEM((2, 9 * CH, CH), F32),
            pltpu.VMEM((2, 9 * CH, CH), BF),
            pltpu.VMEM((2, 9 * CH, CH), BF),
            pltpu.VMEM((TOKENS, CH), F32),
            field,
            field,
            field,
            field,
            field,
            field,
            pltpu.VMEM((MICROS, ROWS + 2, COLS, CH), F32),
            pltpu.VMEM((MICROS, ROWS + 4, COLS, 3 * CH), BF),
            pltpu.VMEM((MICROS, ROWS + 2, COLS, 3 * CH), BF),
            pltpu.VMEM((MICROS, ROWS + 4, COLS, 3 * CH), BF),
            pltpu.VMEM((MICROS, ROWS + 2, COLS, 3 * CH), BF),
            pltpu.VMEM((CH, TOKENS), BF),
            pltpu.VMEM((CH, TOKENS), BF),
            pltpu.VMEM((4, 2, MICROS, 2 * COLS, CH), BF),
            pltpu.VMEM((4, 2, MICROS, 2 * COLS, CH), BF),
            pltpu.VMEM((8, TOKENS), F32),
            pltpu.VMEM((8, CH), F32),
            pltpu.VMEM((7, 8, CH), F32),
            pltpu.VMEM((6, 8, CH), F32),
            pltpu.VMEM((8, CH), F32),
            pltpu.VMEM((8, SLOT, CH), F32),
            pltpu.VMEM((32, SLOT, CH), BF),
            pltpu.VMEM((32, 2, CSLOT, CH), BF),
            dma((8,)),
            dma((32,)),
            dma((32,)),
            dma((32,)),
            dma((32,)),
            dma((4, 2)),
            dma((4, 2)),
            dma((3,)),
            dma((3,)),
            dma((6,)),
            dma((6,)),
            dma((32,)),
            dma((32,)),
            dma((32,)),
            dma((32,)),
            pltpu.SemaphoreType.REGULAR,
        ],
        compiler_params=pltpu.CompilerParams(
            collective_id=0, has_side_effects=True, vmem_limit_bytes=60 * 1024 * 1024
        ),
        cost_estimate=pl.CostEstimate(
            flops=15_000_000_000, bytes_accessed=14_000_000, transcendentals=1_000_000
        ),
        name="main_kernel",
    )(hooks, proj, conv, head, light, illum, offsets, photos)


def body(hooks, proj_weight, conv_weight, head_weight, light_color, illum, offsets, photos):
    npix = 3 * MICROS * lax.axis_size("dp") * ROWS * lax.axis_size("fsdp") * COLS
    factor = 2.0 * LOSS_SCALE / npix
    tokens = hooks.reshape(TOKENS, D)
    grad_proj, grad_conv, total = run_main(
        factor, tokens, proj_weight[0], conv_weight[0], head_weight, light_color.T,
        illum, offsets.transpose(0, 2, 1), photos,
    )
    return (grad_proj[None], grad_conv[None], total[:3], total[3, 0] / npix)


def solution(mesh):
    placed = (
        P("segment", "dp", "fsdp", None, None),
        P("segment", "fsdp", None),
        P("segment", None, "fsdp", None),
        P(),
        P(),
        P("dp", None),
        P("dp", None, None),
        P("dp", None, None, None, None),
    )
    return jax.shard_map(
        body,
        mesh=mesh,
        in_specs=placed,
        out_specs=(P("segment", "fsdp", None), P("segment", None, "fsdp", None), P(), P()),
        check_vma=False,
    )
```

```python
import functools

import jax
import jax.numpy as jnp
from jax import lax
from jax.experimental import pallas as pl
from jax.experimental.pallas import tpu as pltpu
from jax.sharding import PartitionSpec as P

LOSS_SCALE = 8192.0
MESH = pl.DeviceIdType.MESH
BF = jnp.bfloat16
F32 = jnp.float32

MICROS, ROWS, COLS, CH = 2, 8, 64, 256
TOKENS = MICROS * ROWS * COLS
HALF = ROWS * COLS
D = 6144
SLOT = 192
CSLOT = 72
CHUNK = 4 * SLOT

SIDE = (1, -1)
ACROSS = (1, -1, 2)
PLANE = [(1, 0), (-1, 0), (2, 0), (0, 1), (2, 1)]
GREET = PLANE + [(1, 1), (-1, 1)]
ORDER = [(0, 0)] + PLANE + [(1, 1), (-1, 1)]
BACK = [(1, 1), (-1, 1), (2, 0), (2, 1), (1, 0), (-1, 0), (0, 1), (0, 0)]
QUEUE = BACK[2:]


def place():
    f = lax.axis_index("fsdp")
    return f // 8, (f // 4) % 2, f % 4


def at(x, y, z):
    return {"fsdp": x * 8 + y * 4 + z}


def dot(a, b, dims=((1,), (0,))):
    return lax.dot_general(a, b, (dims, ((), ())), preferred_element_type=F32)


def gelu_parts(v):
    c = 0.7978845608028654
    t = jnp.tanh(c * (v + 0.044715 * (v * v * v)))
    return t


def gelu(v):
    return 0.5 * v * (1.0 + gelu_parts(v))


def gelu_slope(v):
    c = 0.7978845608028654
    t = gelu_parts(v)
    return 0.5 * (1.0 + t) + 0.5 * v * (1.0 - t * t) * (c * (1.0 + 3.0 * 0.044715 * (v * v)))


class Axis:
    def __init__(self, p_is_x):
        x, y, z = place()
        self.p_is_x = p_is_x
        self.p, self.y, self.q = (x, y, z) if p_is_x else (z, y, x)

    def coords(self, dp, r, dq):
        p = (self.p + (dp + 4)) % 4
        q = (self.q + (dq + 4)) % 4
        y = (self.y + r) % 2
        return (p, y, q) if self.p_is_x else (q, y, p)

    def slot(self, dp, r, dq):
        x, y, z = self.coords(dp, r, dq)
        return x * 8 + y * 4 + z

    def device(self, dp, r, dq):
        return at(*self.coords(dp, r, dq))

    def beside(self, dp):
        device = self.device(0, 1, 0)
        return device if dp == 1 else {"dp": 1 - lax.axis_index("dp"), **device}


def rel(dp, r, dq):
    return ((dp % 4) * 2 + r) * 4 + dq % 4


class Gather:
    def __init__(self, axis, buf, send, recv):
        self.a, self.buf, self.send, self.recv = axis, buf, send, recv
        self.copies = []

    def put(self, dp, r, dq, to, device=None):
        tp, tr, tq = to
        a = self.a
        slot = a.slot(dp, r, dq)
        copy = pltpu.make_async_remote_copy(
            src_ref=self.buf.at[slot],
            dst_ref=self.buf.at[slot],
            send_sem=self.send.at[len(self.copies)],
            recv_sem=self.recv.at[rel(dp - tp, (r + tr) % 2, dq - tq)],
            device_id=a.device(tp, tr, tq) if device is None else device,
            device_id_type=MESH,
        )
        copy.start()
        self.copies.append(copy)

    def await_(self, dp, r, dq):
        a = self.a
        slot = a.slot(dp, r, dq)
        pltpu.make_async_remote_copy(
            src_ref=self.buf.at[slot],
            dst_ref=self.buf.at[slot],
            send_sem=self.send.at[0],
            recv_sem=self.recv.at[rel(dp, r, dq)],
            device_id=a.device(0, 1, 0),
            device_id_type=MESH,
        ).wait_recv()

    def spread(self):
        for dp, r in PLANE:
            self.put(0, 0, 0, (-dp, r, 0))

    def along(self, dp, r):
        if (dp, r) != (0, 0):
            self.await_(dp, r, 0)
        for dq in ACROSS:
            self.put(dp, r, 0, (0, 0, dq))
        if r == 0 and dp in SIDE:
            self.put(dp, 0, 0, (0, 1, 0), self.a.beside(dp))

    def sideways(self, dq):
        for dp in SIDE:
            self.await_(dp, 0, dq)
            self.put(dp, 0, dq, (0, 1, 0), self.a.beside(dp))

    def last(self, dp, r):
        if r == 1 and dp in SIDE:
            for dq in (0,) + ACROSS:
                self.await_(dp, r, dq)
        elif r == 1 or dp not in SIDE:
            for dq in ACROSS:
                self.await_(dp, r, dq)

    def drain(self):
        for copy in self.copies:
            copy.wait_send()


def entry_barrier(devices):
    barrier = pltpu.get_barrier_semaphore()
    for device in devices:
        pl.semaphore_signal(barrier, inc=1, device_id=device, device_id_type=MESH)
    pl.semaphore_wait(barrier, len(devices))


def partners():
    pa, pc = Axis(True), Axis(False)
    return [pa.device(dp, r, 0) for dp, r in GREET] + [
        pc.device(dp, r, 0) for dp, r in GREET if dp != 0
    ]


def load_rows(source, target, sem):
    copies = []
    for i in range(8):
        rows = pl.ds(i * (TOKENS // 8), TOKENS // 8)
        copy = pltpu.make_async_copy(source.at[rows, :], target.at[rows, :], sem.at[i])
        copy.start()
        copies.append(copy)
    return copies


def shift_parts(v):
    n = v.shape[0]
    col = lax.broadcasted_iota(jnp.int32, v.shape, 0) % COLS
    before = jnp.where(col == 0, 0.0, pltpu.roll(v, 1, 0))
    after = jnp.where(col == COLS - 1, 0.0, pltpu.roll(v, n - 1, 0))
    return before.astype(BF), v.astype(BF), after.astype(BF)


class Reduce:
    def __init__(self, axis, own, store, stage, got, send, recv, placed=False):
        self.a = axis
        self.own, self.store = own, store
        self.stage, self.got, self.send, self.recv = stage, got, send, recv
        self.placed = placed
        self.copies = []

    def put(self, k, value, device):
        if value is not None:
            self.stage[k] = value.astype(BF)
        copy = pltpu.make_async_remote_copy(
            src_ref=self.stage.at[k],
            dst_ref=self.got.at[k],
            send_sem=self.send.at[k],
            recv_sem=self.recv.at[k],
            device_id=device,
            device_id_type=MESH,
        )
        copy.start()
        self.copies.append(copy)

    def take(self, k):
        pltpu.make_async_remote_copy(
            src_ref=self.stage.at[k],
            dst_ref=self.got.at[k],
            send_sem=self.send.at[k],
            recv_sem=self.recv.at[k],
            device_id=self.a.device(0, 1, 0),
            device_id_type=MESH,
        ).wait_recv()
        return self.got[k].astype(F32)

    def part(self, dp, r, dq):
        return self.own(self.a.slot(dp, r, dq), dp, r, dq)

    def summed(self, dp, r, dq):
        value = self.part(dp, r, dq)
        if r == 0 and dp in SIDE:
            value = value + self.take(side_slot(dp, dq))
        return value

    def first(self, dp, r):
        if r == 1 and dp in SIDE:
            for dq in ACROSS + (0,):
                value = None if self.placed else self.part(dp, r, dq)
                self.put(side_slot(dp, dq), value, self.a.beside(dp))
        else:
            ready = self.placed and not (r == 0 and dp in SIDE)
            for dq in ACROSS:
                value = None if ready else self.summed(dp, r, dq)
                self.put(queue_slot(dp, r, dq), value, self.a.device(0, 0, dq))

    def second(self, dp, r):
        total = self.summed(dp, r, 0)
        for dq in ACROSS:
            total = total + self.take(queue_slot(dp, r, dq))
        if (dp, r) == (0, 0):
            self.kept = total
        else:
            self.put(26 + PLANE.index((dp, r)), total, self.a.device(dp, r, 0))

    def third(self):
        for i in range(len(PLANE)):
            self.kept = self.kept + self.take(26 + i)
        self.put(31, self.kept, {"dp": 1 - lax.axis_index("dp")})

    def fourth(self):
        self.store(self.stage[31].astype(F32) + self.take(31))
        for copy in self.copies:
            copy.wait_send()


def side_slot(dp, dq):
    return SIDE.index(dp) * 4 + dq % 4


def queue_slot(dp, r, dq):
    return 8 + QUEUE.index((dp, r)) * 3 + ACROSS.index(dq)


def part_slot(dp, r, dq):
    if dq == 0:
        return QUEUE.index((dp, r))
    return 6 + SIDE.index(dp) * 3 + ACROSS.index(dq)


def main_kernel(
    factor,
    hooks_ref,
    proj_ref,
    conv_ref,
    head_ref,
    light_ref,
    illum_ref,
    offsets_ref,
    photos_ref,
    proj_out,
    conv_out,
    total_ref,
    hooks_v,
    wproj,
    wconv,
    wf32,
    wbf,
    wflip,
    acc,
    section_in,
    inc,
    out,
    og_in,
    og,
    grad,
    hidden,
    cat_a,
    cat_b,
    cat_c,
    cat_d,
    x1t,
    x2t,
    hsend,
    hrecv,
    targets,
    head_pad,
    hsum,
    hgot,
    hfin,
    part,
    pgot,
    cgot,
    load_sem,
    psend,
    precv,
    csend,
    crecv,
    hs_sem,
    hr_sem,
    seg_s,
    seg_r,
    sum_s,
    sum_r,
    rps,
    rpr,
    rcs,
    rcr,
    gate,
):
    x, y, z = place()
    seg = lax.axis_index("segment")
    dpi = lax.axis_index("dp")
    band = y * 4 + z
    sibling = {"segment": 1 - seg}
    dp_peer = {"dp": 1 - dpi}
    up_j, down_j = (band + 7) % 8, (band + 1) % 8
    up = at(x, up_j // 4, up_j % 4)
    down = at(x, down_j // 4, down_j % 4)
    up_other = {"segment": 1 - seg, **up}
    down_other = {"segment": 1 - seg, **down}

    pa = Axis(True)
    loads = load_rows(hooks_ref, hooks_v, load_sem)

    me = x * 8 + y * 4 + z
    wproj[me] = proj_ref[...]
    wconv[me] = conv_ref[...]

    z1 = at(x, y, z + 1 - 2 * (z % 2))
    z2 = at(x, y, (z + 2) % 4)
    x1 = at(x + 1 - 2 * (x % 2), y, z)
    x2 = at((x + 2) % 4, y, z)
    y1 = at(x, 1 - y, z)
    entry_barrier(partners() + [sibling, dp_peer, up_other, down_other, pa.beside(-1)])

    gp = Gather(pa, wproj, psend, precv)
    gc = Gather(Axis(False), wconv, csend, crecv)

    @pl.when(seg == 1)
    def _():
        pl.semaphore_wait(gate, 1)

    gp.spread()
    gc.spread()
    gp.along(0, 0)
    gc.along(0, 0)

    yy = lax.broadcasted_iota(jnp.int32, (96, HALF), 0)
    nn = lax.broadcasted_iota(jnp.int32, (96, HALF), 1)
    row8 = lax.broadcasted_iota(jnp.int32, (8, HALF), 0)
    for m in range(MICROS):
        oy = offsets_ref[m, 0, x]
        ox = offsets_ref[m, 1, x]
        pick_col = (yy == ox + nn % COLS).astype(F32).astype(BF)
        pick_row = yy == oy + band * ROWS + nn // COLS
        block = jnp.zeros((8, HALF), F32)
        for c in range(3):
            q = dot(photos_ref[m, x, c], pick_col)
            line = jnp.sum(jnp.where(pick_row, q, 0.0), axis=0, keepdims=True)
            block = jnp.where(row8 == c, line, block)
        targets[:, m * HALF : (m + 1) * HALF] = block
    head_pad[...] = jnp.zeros((8, CH), F32)
    head_pad[0:3, :] = head_ref[...].astype(F32)

    acc[...] = jnp.zeros_like(acc)
    for copy in loads:
        copy.wait()

    def project(i):
        dp, r = ORDER[i]
        xs, ys, _ = pa.coords(dp, r, 0)
        base = xs * 8 + ys * 4
        lanes = pl.ds(pl.multiple_of(base * SLOT, CHUNK), CHUNK)
        w = wproj[pl.ds(base, 4)].reshape(CHUNK, CH)

        def step(t, _):
            rows = pl.ds(pl.multiple_of(t * 256, 256), 256)
            acc[rows, :] += dot(hooks_v[rows, lanes], w)
            return 0

        lax.fori_loop(0, TOKENS // 256, step, 0)

    for dp, r in PLANE:
        gp.along(dp, r)
        gc.along(dp, r)
    for dq in ACROSS:
        gp.sideways(dq)
        gc.sideways(dq)

    @pl.when(seg == 0)
    def _():
        pl.semaphore_signal(gate, inc=1, device_id=sibling, device_id_type=MESH)

    for i in range(6):
        gp.last(*ORDER[i])
        project(i)
    for dp, r in ORDER:
        gc.last(dp, r)

    def gather_rows(k, _):
        start = pl.multiple_of(k * CSLOT, 8)
        wf32[0, pl.ds(start, CSLOT), :] = wconv[k, 0].astype(F32)
        wf32[1, pl.ds(start, CSLOT), :] = wconv[k, 1].astype(F32)
        return 0

    lax.fori_loop(0, 32, gather_rows, 0)

    def to_bf(k, _):
        start = pl.multiple_of(k * CH, CH)
        wbf[0, pl.ds(start, CH), :] = wf32[0, pl.ds(start, CH), :].astype(BF)
        wbf[1, pl.ds(start, CH), :] = wf32[1, pl.ds(start, CH), :].astype(BF)
        return 0

    lax.fori_loop(0, 9, to_bf, 0)
    for i in (6, 7):
        gp.last(*ORDER[i])
        project(i)

    def flip_weights():
        def step(k, _):
            source = pl.ds(pl.multiple_of(k * CH, CH), CH)
            target = pl.ds(pl.multiple_of((8 - k) * CH, CH), CH)
            wflip[0, target, :] = wf32[0, source, :].T.astype(BF)
            wflip[1, target, :] = wf32[1, source, :].T.astype(BF)
            return 0

        lax.fori_loop(0, 9, step, 0)

    def seg_copy(src, dst, k):
        return pltpu.make_async_remote_copy(
            src_ref=src,
            dst_ref=dst,
            send_sem=seg_s.at[k],
            recv_sem=seg_r.at[k],
            device_id=sibling,
            device_id_type=MESH,
        )

    def halo(e, side, device):
        return pltpu.make_async_remote_copy(
            src_ref=hsend.at[e, side],
            dst_ref=hrecv.at[e, 1 - side],
            send_sem=hs_sem.at[e, side],
            recv_sem=hr_sem.at[e, 1 - side],
            device_id=device,
            device_id_type=MESH,
        )

    def halo_start(e, to_up, to_down):
        halo(e, 0, to_up).start()
        halo(e, 1, to_down).start()

    def halo_sent(e):
        halo(e, 0, up).wait_send()
        halo(e, 1, up).wait_send()

    def halo_here(e):
        halo(e, 0, up).wait_recv()
        halo(e, 1, up).wait_recv()

    def edges(e, source):
        for m in range(MICROS):
            hsend[e, 0, m] = source[m * HALF : m * HALF + 2 * COLS, :]
            hsend[e, 1, m] = source[(m + 1) * HALF - 2 * COLS : (m + 1) * HALF, :]

    def fill(cat, m, row, value):
        a, b, c = shift_parts(value)
        n = value.shape[0] // COLS
        cat[m, row : row + n, :, 0:CH] = a.reshape(n, COLS, CH)
        cat[m, row : row + n, :, CH : 2 * CH] = b.reshape(n, COLS, CH)
        cat[m, row : row + n, :, 2 * CH : 3 * CH] = c.reshape(n, COLS, CH)

    def tokens_of(m):
        return slice(m * HALF, (m + 1) * HALF)

    def conv(weights, which, left):
        total = None
        for ky in range(3):
            value = left(ky)
            value = value.reshape(-1, 3 * CH)
            piece = dot(value, weights[which, ky * 3 * CH : (ky + 1) * 3 * CH, :])
            total = piece if total is None else total + piece
        return total

    def conv_weight_grad(xt, cat, low, which):
        for ky in range(3):
            total = None
            for m in range(MICROS):
                right = cat[m, low - ky : low - ky + ROWS].reshape(HALF, 3 * CH)
                piece = dot(xt[:, tokens_of(m)], right)
                total = piece if total is None else total + piece
            for kx in range(3):
                j = 2 - kx
                row = (3 * ky + kx) * CH
                wf32[which, row : row + CH, :] = total[:, j * CH : (j + 1) * CH]

    def two_convs(cat, weights, first, middle, mid, second, halo_ready):
        for m in range(MICROS):
            v = conv(weights, first, lambda ky: cat[m, 2 + ky : 8 + ky])
            fill(mid, m, 2, middle(m, 1, 6, v))
        halo_ready()
        for low, edge in ((0, 0), (8, 7)):
            v = conv(weights, first, lambda ky: cat[:, low + ky : low + ky + 2])
            for m in range(MICROS):
                u = middle(m, low - 1, 2, v[m * 2 * COLS : (m + 1) * 2 * COLS])
                outer = lax.broadcasted_iota(jnp.int32, u.shape, 0) // COLS == edge // 7
                u = jnp.where(jnp.logical_and(outer, band == edge), 0.0, u)
                fill(mid, m, low, u)
        return [conv(weights, second, lambda ky, m=m: mid[m, ky : ky + ROWS]) for m in range(MICROS)]

    def halo_rows(cat, rows_of):
        for side, row, last in ((0, 0, 0), (1, ROWS + 2, 7)):
            for m in range(MICROS):
                v = rows_of(side, m)
                v = jnp.where(band == last, jnp.zeros_like(v), v)
                fill(cat, m, row, v)

    section_in[...] = acc[...].astype(BF)
    edges(0, section_in)
    halo_start(0, up, down)
    gp.drain()
    gc.drain()

    @pl.when(seg == 1)
    def _():
        flip_weights()
        seg_copy(out, inc, 0).wait_recv()
        section_in[...] = (section_in[...].astype(F32) + inc[...].astype(F32)).astype(BF)

    for m in range(MICROS):
        fill(cat_a, m, 2, gelu(section_in[tokens_of(m), :].astype(F32)).astype(BF).astype(F32))

    def forward_halo():
        halo_here(0)

        @pl.when(seg == 1)
        def _():
            halo_here(1)

        def rows_of(side, m):
            shape = (2 * COLS, CH)
            more = jnp.where(seg == 1, hrecv[1, side, m].astype(F32), 0.0)
            v = (hrecv[0, side, m].astype(F32) + more).astype(BF).astype(F32)
            return gelu(v).astype(BF).astype(F32)

        halo_rows(cat_a, rows_of)

    def keep_hidden(m, row, n, v):
        hidden[m, row + 1 : row + 1 + n] = v.reshape(n, COLS, CH)
        return gelu(v).astype(BF).astype(F32)

    update = two_convs(cat_a, wbf, 0, keep_hidden, cat_b, 1, forward_halo)
    for m in range(MICROS):
        out[tokens_of(m), :] = (section_in[tokens_of(m), :].astype(F32) + update[m]).astype(BF)

    def transposes():
        for m in range(MICROS):
            v = cat_a[m, 2 : 2 + ROWS, :, CH : 2 * CH].reshape(HALF, CH).astype(F32)
            x1t[:, tokens_of(m)] = v.T.astype(BF)
            v = cat_b[m, 1 : 1 + ROWS, :, CH : 2 * CH].reshape(HALF, CH).astype(F32)
            x2t[:, tokens_of(m)] = v.T.astype(BF)

    def sum_copy(k, device):
        return pltpu.make_async_remote_copy(
            src_ref=hsum.at[k],
            dst_ref=hgot.at[k],
            send_sem=sum_s.at[k],
            recv_sem=sum_r.at[k],
            device_id=device,
            device_id_type=MESH,
        )

    rounds = [y1, dp_peer, z1, z2, x1, x2]

    def sum_start(k):
        @pl.when(seg == 1)
        def _():
            sum_copy(k, rounds[k]).start()

    def sum_end(k):
        @pl.when(seg == 1)
        def _():
            sum_copy(k, rounds[k]).wait()
            hsum[k + 1] = hsum[k] + hgot[k]

    @pl.when(seg == 0)
    def _():
        edges(1, out)
        halo_start(1, up_other, down_other)
        to_next = seg_copy(out, inc, 0)
        to_next.start()
        flip_weights()
        transposes()
        to_next.wait_send()
        halo_sent(1)
        seg_copy(grad, og_in, 1).wait_recv()
        og[...] = og_in[...]

    @pl.when(seg == 1)
    def _():
        hw = head_pad[...].astype(BF)
        o = out[...]
        logits = dot(hw, o, ((1,), (1,)))
        albedo = 1.0 / (1.0 + jnp.exp(-logits))
        row = lax.broadcasted_iota(jnp.int32, (8, TOKENS), 0)
        lane = lax.broadcasted_iota(jnp.int32, (8, TOKENS), 1)
        tint = jnp.zeros((8, TOKENS), F32)
        for m in range(MICROS):
            light = illum_ref[m, x]
            for c in range(3):
                tint = jnp.where((row == c) & (lane // HALF == m), light_ref[c, light], tint)
        mismatch = albedo * tint - targets[...]
        lg = (factor * mismatch * tint * albedo * (1.0 - albedo)).astype(BF)
        lgt = lg.astype(F32).T.astype(BF)
        og[...] = dot(lgt, hw).astype(BF)
        edges(2, og)
        halo_start(2, up, down)
        squares = jnp.sum(mismatch * mismatch)
        hg = dot(lg, o)
        row_h = lax.broadcasted_iota(jnp.int32, (8, CH), 0)
        hsum[0] = jnp.where(row_h == 3, squares, hg)

    sum_start(0)

    for m in range(MICROS):
        fill(cat_c, m, 2, og[tokens_of(m), :].astype(F32))

    def backward_halo():
        @pl.when(seg == 1)
        def _():
            halo_here(2)

        @pl.when(seg == 0)
        def _():
            halo_here(3)

        def rows_of(side, m):
            v = jnp.where(seg == 1, hrecv[2, side, m].astype(F32), hrecv[3, side, m].astype(F32))
            return v

        halo_rows(cat_c, rows_of)

    def through(m, row, n, v):
        h = hidden[m, row + 1 : row + 1 + n].reshape(n * COLS, CH)
        return (v * gelu_slope(h)).astype(BF).astype(F32)

    back = two_convs(cat_c, wflip, 1, through, cat_d, 0, backward_halo)
    for m in range(MICROS):
        rows = tokens_of(m)
        slope = gelu_slope(section_in[rows, :].astype(F32))
        grad[rows, :] = (og[rows, :].astype(F32) + back[m] * slope).astype(BF)

    @pl.when(seg == 1)
    def _():
        edges(3, grad)
        halo_start(3, up_other, down_other)
        seg_copy(grad, og_in, 1).start()
        transposes()

    sum_end(0)
    sum_start(1)
    conv_weight_grad(x2t, cat_c, 3, 1)
    sum_end(1)
    sum_start(2)
    conv_weight_grad(x1t, cat_d, 2, 0)
    sum_end(2)
    sum_start(3)

    def own_conv(slot, dp, r, dq):
        start = pl.multiple_of(slot * CSLOT, 8)
        return wf32[:, pl.ds(start, CSLOT), :]

    def own_proj(slot, dp, r, dq):
        return part[part_slot(dp, r, dq)]

    def store_conv(v):
        conv_out[...] = v

    def store_proj(v):
        proj_out[...] = v

    rc = Reduce(Axis(False), own_conv, store_conv, wconv, cgot, rcs, rcr)
    rp = Reduce(pa, own_proj, store_proj, wproj, pgot, rps, rpr, placed=True)

    def compute(dp, r):
        xs, ys, _ = pa.coords(dp, r, 0)
        base = xs * 8 + ys * 4
        lanes = pl.ds(pl.multiple_of(base * SLOT, CHUNK), CHUNK)
        v = dot(hooks_v[:, lanes], grad[...], ((0,), (0,)))
        for k in range(4):
            ahead = (k - z + 4) % 4
            block = v[k * SLOT : (k + 1) * SLOT]
            for dq in (0,) + ACROSS:

                @pl.when(ahead == dq % 4)
                def _():
                    if r == 1 and dp in SIDE:
                        wproj[side_slot(dp, dq)] = block.astype(BF)
                    elif dq == 0 or (r == 0 and dp in SIDE):
                        part[part_slot(dp, r, dq)] = block
                    else:
                        wproj[queue_slot(dp, r, dq)] = block.astype(BF)

    for i, (dp, r) in enumerate(BACK):
        rc.first(dp, r)
        compute(dp, r)
        rp.first(dp, r)
        if i in (1, 3, 5):
            sum_end(3 + i // 2)
            if i < 5:
                sum_start(4 + i // 2)
        if i >= 4:
            rc.second(*BACK[i - 2])
            rp.second(*BACK[i - 2])
    final = pltpu.make_async_remote_copy(
        src_ref=hsum.at[6],
        dst_ref=hfin,
        send_sem=seg_s.at[2],
        recv_sem=seg_r.at[2],
        device_id=sibling,
        device_id_type=MESH,
    )

    @pl.when(seg == 1)
    def _():
        final.start()
        total_ref[...] = hsum[6]

    for dp, r in BACK[6:]:
        rc.second(dp, r)
        rp.second(dp, r)
    rc.third()
    rp.third()
    rc.fourth()
    rp.fourth()
    halo_sent(0)

    @pl.when(seg == 1)
    def _():
        halo_sent(2)
        halo_sent(3)
        seg_copy(grad, og_in, 1).wait_send()
        final.wait_send()

    @pl.when(seg == 0)
    def _():
        final.wait_recv()
        total_ref[...] = hfin[...]


def run_main(factor, hooks, proj, conv, head, light, illum, offsets, photos):
    vm = pl.BlockSpec(memory_space=pltpu.VMEM)
    sm = pl.BlockSpec(memory_space=pltpu.SMEM)
    dma = pltpu.SemaphoreType.DMA
    field = pltpu.VMEM((TOKENS, CH), BF)
    return pl.pallas_call(
        functools.partial(main_kernel, factor),
        out_shape=(
            jax.ShapeDtypeStruct((SLOT, CH), F32),
            jax.ShapeDtypeStruct((2, CSLOT, CH), F32),
            jax.ShapeDtypeStruct((8, CH), F32),
        ),
        in_specs=[pl.BlockSpec(memory_space=pl.ANY), vm, vm, vm, sm, sm, sm, vm],
        out_specs=(vm, vm, vm),
        scratch_shapes=[
            pltpu.VMEM((TOKENS, D), BF),
            pltpu.VMEM((32, SLOT, CH), BF),
            pltpu.VMEM((32, 2, CSLOT, CH), BF),
            pltpu.VMEM((2, 9 * CH, CH), F32),
            pltpu.VMEM((2, 9 * CH, CH), BF),
            pltpu.VMEM((2, 9 * CH, CH), BF),
            pltpu.VMEM((TOKENS, CH), F32),
            field,
            field,
            field,
            field,
            field,
            field,
            pltpu.VMEM((MICROS, ROWS + 2, COLS, CH), F32),
            pltpu.VMEM((MICROS, ROWS + 4, COLS, 3 * CH), BF),
            pltpu.VMEM((MICROS, ROWS + 2, COLS, 3 * CH), BF),
            pltpu.VMEM((MICROS, ROWS + 4, COLS, 3 * CH), BF),
            pltpu.VMEM((MICROS, ROWS + 2, COLS, 3 * CH), BF),
            pltpu.VMEM((CH, TOKENS), BF),
            pltpu.VMEM((CH, TOKENS), BF),
            pltpu.VMEM((4, 2, MICROS, 2 * COLS, CH), BF),
            pltpu.VMEM((4, 2, MICROS, 2 * COLS, CH), BF),
            pltpu.VMEM((8, TOKENS), F32),
            pltpu.VMEM((8, CH), F32),
            pltpu.VMEM((7, 8, CH), F32),
            pltpu.VMEM((6, 8, CH), F32),
            pltpu.VMEM((8, CH), F32),
            pltpu.VMEM((12, SLOT, CH), F32),
            pltpu.VMEM((32, SLOT, CH), BF),
            pltpu.VMEM((32, 2, CSLOT, CH), BF),
            dma((8,)),
            dma((32,)),
            dma((32,)),
            dma((32,)),
            dma((32,)),
            dma((4, 2)),
            dma((4, 2)),
            dma((3,)),
            dma((3,)),
            dma((6,)),
            dma((6,)),
            dma((32,)),
            dma((32,)),
            dma((32,)),
            dma((32,)),
            pltpu.SemaphoreType.REGULAR,
        ],
        compiler_params=pltpu.CompilerParams(
            collective_id=0, has_side_effects=True, vmem_limit_bytes=60 * 1024 * 1024
        ),
        cost_estimate=pl.CostEstimate(
            flops=15_000_000_000, bytes_accessed=14_000_000, transcendentals=1_000_000
        ),
        name="main_kernel",
    )(hooks, proj, conv, head, light, illum, offsets, photos)


def finish_kernel(npix, proj_ref, conv_ref, total_ref, proj_out, conv_out, head_out, loss_out):
    proj_out[...] = proj_ref[...]
    conv_out[...] = conv_ref[...]
    head_out[...] = total_ref[0:3, :]
    loss_out[...] = total_ref[3:4, 0:1] / npix


def run_finish(npix, proj, conv, total):
    vm = pl.BlockSpec(memory_space=pltpu.VMEM)
    return pl.pallas_call(
        functools.partial(finish_kernel, npix),
        out_shape=(
            jax.ShapeDtypeStruct((SLOT, CH), F32),
            jax.ShapeDtypeStruct((2, CSLOT, CH), F32),
            jax.ShapeDtypeStruct((3, CH), F32),
            jax.ShapeDtypeStruct((1, 1), F32),
        ),
        in_specs=[vm, vm, vm],
        out_specs=(vm, vm, vm, vm),
        name="finish_kernel",
    )(proj, conv, total)


def body(hooks, proj_weight, conv_weight, head_weight, light_color, illum, offsets, photos):
    npix = 3 * MICROS * lax.axis_size("dp") * ROWS * lax.axis_size("fsdp") * COLS
    factor = 2.0 * LOSS_SCALE / npix
    tokens = hooks.reshape(TOKENS, D)
    grad_proj, grad_conv, total = run_main(
        factor, tokens, proj_weight[0], conv_weight[0], head_weight, light_color.T,
        illum, offsets.transpose(0, 2, 1), photos,
    )
    grad_proj, grad_conv, head, loss = run_finish(npix, grad_proj, grad_conv, total)
    return (grad_proj[None], grad_conv[None], head, loss[0, 0])


def solution(mesh):
    placed = (
        P("segment", "dp", "fsdp", None, None),
        P("segment", "fsdp", None),
        P("segment", None, "fsdp", None),
        P(),
        P(),
        P("dp", None),
        P("dp", None, None),
        P("dp", None, None, None, None),
    )
    return jax.shard_map(
        body,
        mesh=mesh,
        in_specs=placed,
        out_specs=(P("segment", "fsdp", None), P("segment", None, "fsdp", None), P(), P()),
        check_vma=False,
    )
```

```python
import functools

import jax
import jax.numpy as jnp
from jax import lax
from jax.experimental import pallas as pl
from jax.experimental.pallas import tpu as pltpu
from jax.sharding import PartitionSpec as P

LOSS_SCALE = 8192.0
MESH = pl.DeviceIdType.MESH
BF = jnp.bfloat16
F32 = jnp.float32

MICROS, ROWS, COLS, CH = 2, 8, 64, 256
TOKENS = MICROS * ROWS * COLS
HALF = ROWS * COLS
D = 6144
SLOT = 192
CSLOT = 72
CHUNK = 4 * SLOT

SIDE = (1, -1)
ACROSS = (1, -1, 2)
PLANE = [(1, 0), (-1, 0), (2, 0), (0, 1), (2, 1)]
GREET = PLANE + [(1, 1), (-1, 1)]
ORDER = [(0, 0)] + PLANE + [(1, 1), (-1, 1)]
BACK = [(1, 1), (-1, 1), (2, 0), (2, 1), (1, 0), (-1, 0), (0, 1), (0, 0)]
QUEUE = BACK[2:]


def place():
    f = lax.axis_index("fsdp")
    return f // 8, (f // 4) % 2, f % 4


def at(x, y, z):
    return {"fsdp": x * 8 + y * 4 + z}


def dot(a, b, dims=((1,), (0,))):
    return lax.dot_general(a, b, (dims, ((), ())), preferred_element_type=F32)


def gelu_parts(v):
    c = 0.7978845608028654
    t = jnp.tanh(c * (v + 0.044715 * (v * v * v)))
    return t


def gelu(v):
    return 0.5 * v * (1.0 + gelu_parts(v))


def gelu_slope(v):
    c = 0.7978845608028654
    t = gelu_parts(v)
    return 0.5 * (1.0 + t) + 0.5 * v * (1.0 - t * t) * (c * (1.0 + 3.0 * 0.044715 * (v * v)))


class Axis:
    def __init__(self, p_is_x):
        x, y, z = place()
        self.p_is_x = p_is_x
        self.p, self.y, self.q = (x, y, z) if p_is_x else (z, y, x)

    def coords(self, dp, r, dq):
        p = (self.p + (dp + 4)) % 4
        q = (self.q + (dq + 4)) % 4
        y = (self.y + r) % 2
        return (p, y, q) if self.p_is_x else (q, y, p)

    def slot(self, dp, r, dq):
        x, y, z = self.coords(dp, r, dq)
        return x * 8 + y * 4 + z

    def device(self, dp, r, dq):
        return at(*self.coords(dp, r, dq))

    def beside(self, dp):
        device = self.device(0, 1, 0)
        return device if dp == 1 else {"dp": 1 - lax.axis_index("dp"), **device}


def rel(dp, r, dq):
    return ((dp % 4) * 2 + r) * 4 + dq % 4


class Gather:
    def __init__(self, axis, buf, send, recv):
        self.a, self.buf, self.send, self.recv = axis, buf, send, recv
        self.copies = []

    def put(self, dp, r, dq, to, device=None):
        tp, tr, tq = to
        a = self.a
        slot = a.slot(dp, r, dq)
        copy = pltpu.make_async_remote_copy(
            src_ref=self.buf.at[slot],
            dst_ref=self.buf.at[slot],
            send_sem=self.send.at[len(self.copies)],
            recv_sem=self.recv.at[rel(dp - tp, (r + tr) % 2, dq - tq)],
            device_id=a.device(tp, tr, tq) if device is None else device,
            device_id_type=MESH,
        )
        copy.start()
        self.copies.append(copy)

    def await_(self, dp, r, dq):
        a = self.a
        slot = a.slot(dp, r, dq)
        pltpu.make_async_remote_copy(
            src_ref=self.buf.at[slot],
            dst_ref=self.buf.at[slot],
            send_sem=self.send.at[0],
            recv_sem=self.recv.at[rel(dp, r, dq)],
            device_id=a.device(0, 1, 0),
            device_id_type=MESH,
        ).wait_recv()

    def spread(self):
        for dp, r in PLANE:
            self.put(0, 0, 0, (-dp, r, 0))

    def along(self, dp, r):
        if (dp, r) != (0, 0):
            self.await_(dp, r, 0)
        for dq in ACROSS:
            self.put(dp, r, 0, (0, 0, dq))
        if r == 0 and dp in SIDE:
            self.put(dp, 0, 0, (0, 1, 0), self.a.beside(dp))

    def sideways(self, dq):
        for dp in SIDE:
            self.await_(dp, 0, dq)
            self.put(dp, 0, dq, (0, 1, 0), self.a.beside(dp))

    def last(self, dp, r):
        if r == 1 and dp in SIDE:
            for dq in (0,) + ACROSS:
                self.await_(dp, r, dq)
        elif r == 1 or dp not in SIDE:
            for dq in ACROSS:
                self.await_(dp, r, dq)

    def drain(self):
        for copy in self.copies:
            copy.wait_send()


def entry_barrier(devices):
    barrier = pltpu.get_barrier_semaphore()
    for device in devices:
        pl.semaphore_signal(barrier, inc=1, device_id=device, device_id_type=MESH)
    pl.semaphore_wait(barrier, len(devices))


def partners():
    pa, pc = Axis(True), Axis(False)
    return [pa.device(dp, r, 0) for dp, r in GREET] + [
        pc.device(dp, r, 0) for dp, r in GREET if dp != 0
    ]


def load_rows(source, target, sem):
    copies = []
    for i in range(8):
        rows = pl.ds(i * (TOKENS // 8), TOKENS // 8)
        copy = pltpu.make_async_copy(source.at[rows, :], target.at[rows, :], sem.at[i])
        copy.start()
        copies.append(copy)
    return copies


def shift_parts(v):
    n = v.shape[0]
    grid = (n // COLS, COLS, CH)
    col = lax.broadcasted_iota(jnp.int32, (1, COLS, CH), 1)
    before = jnp.where(col == 0, 0.0, pltpu.roll(v, 1, 0).reshape(grid))
    after = jnp.where(col == COLS - 1, 0.0, pltpu.roll(v, n - 1, 0).reshape(grid))
    return before.astype(BF), v.reshape(grid).astype(BF), after.astype(BF)


class Reduce:
    def __init__(self, axis, own, store, stage, got, send, recv, placed=False):
        self.a = axis
        self.own, self.store = own, store
        self.stage, self.got, self.send, self.recv = stage, got, send, recv
        self.placed = placed
        self.copies = []

    def put(self, k, value, device):
        if value is not None:
            self.stage[k] = value.astype(BF)
        copy = pltpu.make_async_remote_copy(
            src_ref=self.stage.at[k],
            dst_ref=self.got.at[k],
            send_sem=self.send.at[k],
            recv_sem=self.recv.at[k],
            device_id=device,
            device_id_type=MESH,
        )
        copy.start()
        self.copies.append(copy)

    def take(self, k):
        pltpu.make_async_remote_copy(
            src_ref=self.stage.at[k],
            dst_ref=self.got.at[k],
            send_sem=self.send.at[k],
            recv_sem=self.recv.at[k],
            device_id=self.a.device(0, 1, 0),
            device_id_type=MESH,
        ).wait_recv()
        return self.got[k].astype(F32)

    def part(self, dp, r, dq):
        return self.own(self.a.slot(dp, r, dq), dp, r, dq)

    def summed(self, dp, r, dq):
        value = self.part(dp, r, dq)
        if r == 0 and dp in SIDE:
            value = value + self.take(side_slot(dp, dq))
        return value

    def first(self, dp, r):
        if r == 1 and dp in SIDE:
            for dq in ACROSS + (0,):
                value = None if self.placed else self.part(dp, r, dq)
                self.put(side_slot(dp, dq), value, self.a.beside(dp))
        else:
            ready = self.placed and not (r == 0 and dp in SIDE)
            for dq in ACROSS:
                value = None if ready else self.summed(dp, r, dq)
                self.put(queue_slot(dp, r, dq), value, self.a.device(0, 0, dq))

    def second(self, dp, r):
        total = self.summed(dp, r, 0)
        for dq in ACROSS:
            total = total + self.take(queue_slot(dp, r, dq))
        if (dp, r) == (0, 0):
            self.kept = total
        else:
            self.put(26 + PLANE.index((dp, r)), total, self.a.device(dp, r, 0))

    def third(self):
        for i in range(len(PLANE)):
            self.kept = self.kept + self.take(26 + i)
        self.put(31, self.kept, {"dp": 1 - lax.axis_index("dp")})

    def fourth(self):
        self.store(self.stage[31].astype(F32) + self.take(31))
        for copy in self.copies:
            copy.wait_send()


def side_slot(dp, dq):
    return SIDE.index(dp) * 4 + dq % 4


def queue_slot(dp, r, dq):
    return 8 + QUEUE.index((dp, r)) * 3 + ACROSS.index(dq)


def part_slot(dp, r, dq):
    if dq == 0:
        return QUEUE.index((dp, r))
    return 6 + SIDE.index(dp) * 3 + ACROSS.index(dq)


def main_kernel(
    factor,
    hooks_ref,
    proj_ref,
    conv_ref,
    head_ref,
    light_ref,
    illum_ref,
    offsets_ref,
    photos_ref,
    proj_out,
    conv_out,
    total_ref,
    hooks_v,
    photos_v,
    wproj,
    wconv,
    wf32,
    wbf,
    wflip,
    acc,
    section_in,
    inc,
    out,
    og_in,
    og,
    grad,
    hidden,
    cat_a,
    cat_b,
    cat_c,
    cat_d,
    x1t,
    x2t,
    hsend,
    hrecv,
    targets,
    head_pad,
    hsum,
    hgot,
    hfin,
    part,
    pgot,
    cgot,
    load_sem,
    psend,
    precv,
    csend,
    crecv,
    hs_sem,
    hr_sem,
    seg_s,
    seg_r,
    sum_s,
    sum_r,
    rps,
    rpr,
    rcs,
    rcr,
    gate,
):
    x, y, z = place()
    seg = lax.axis_index("segment")
    dpi = lax.axis_index("dp")
    band = y * 4 + z
    sibling = {"segment": 1 - seg}
    dp_peer = {"dp": 1 - dpi}
    up_j, down_j = (band + 7) % 8, (band + 1) % 8
    up = at(x, up_j // 4, up_j % 4)
    down = at(x, down_j // 4, down_j % 4)
    up_other = {"segment": 1 - seg, **up}
    down_other = {"segment": 1 - seg, **down}

    pa = Axis(True)
    loads = load_rows(hooks_ref, hooks_v, load_sem)
    pictures = []
    for m in range(MICROS):
        copy = pltpu.make_async_copy(photos_ref.at[m, x], photos_v.at[m], load_sem.at[8 + m])
        copy.start()
        pictures.append(copy)

    me = x * 8 + y * 4 + z
    wproj[me] = proj_ref[...]
    wconv[me] = conv_ref[...]

    z1 = at(x, y, z + 1 - 2 * (z % 2))
    z2 = at(x, y, (z + 2) % 4)
    x1 = at(x + 1 - 2 * (x % 2), y, z)
    x2 = at((x + 2) % 4, y, z)
    y1 = at(x, 1 - y, z)
    entry_barrier(partners() + [sibling, dp_peer, up_other, down_other, pa.beside(-1)])

    gp = Gather(pa, wproj, psend, precv)
    gc = Gather(Axis(False), wconv, csend, crecv)

    @pl.when(seg == 1)
    def _():
        pl.semaphore_wait(gate, 1)

    gp.spread()
    gc.spread()
    gp.along(0, 0)
    gc.along(0, 0)

    yy = lax.broadcasted_iota(jnp.int32, (96, HALF), 0)
    nn = lax.broadcasted_iota(jnp.int32, (96, HALF), 1)
    row8 = lax.broadcasted_iota(jnp.int32, (8, HALF), 0)
    for m in range(MICROS):
        pictures[m].wait()
        oy = offsets_ref[m, 0, x]
        ox = offsets_ref[m, 1, x]
        pick_col = (yy == ox + nn % COLS).astype(F32).astype(BF)
        pick_row = yy == oy + band * ROWS + nn // COLS
        block = jnp.zeros((8, HALF), F32)
        for c in range(3):
            q = dot(photos_v[m, c], pick_col)
            line = jnp.sum(jnp.where(pick_row, q, 0.0), axis=0, keepdims=True)
            block = jnp.where(row8 == c, line, block)
        targets[:, m * HALF : (m + 1) * HALF] = block
    head_pad[...] = jnp.zeros((8, CH), F32)
    head_pad[0:3, :] = head_ref[...].astype(F32)

    acc[...] = jnp.zeros_like(acc)
    for copy in loads:
        copy.wait()

    def project(i):
        dp, r = ORDER[i]
        xs, ys, _ = pa.coords(dp, r, 0)
        base = xs * 8 + ys * 4
        lanes = pl.ds(pl.multiple_of(base * SLOT, CHUNK), CHUNK)
        w = wproj[pl.ds(base, 4)].reshape(CHUNK, CH)

        def step(t, _):
            rows = pl.ds(pl.multiple_of(t * 256, 256), 256)
            acc[rows, :] += dot(hooks_v[rows, lanes], w)
            return 0

        lax.fori_loop(0, TOKENS // 256, step, 0)

    for dp, r in PLANE:
        gp.along(dp, r)
        gc.along(dp, r)
    for dq in ACROSS:
        gp.sideways(dq)
        gc.sideways(dq)

    @pl.when(seg == 0)
    def _():
        pl.semaphore_signal(gate, inc=1, device_id=sibling, device_id_type=MESH)

    pc = gc.a

    def gather_rows(dp, r):
        for dq in (0,) + ACROSS:
            k = pc.slot(dp, r, dq)
            rows = pl.ds(pl.multiple_of(k * CSLOT, 8), CSLOT)
            wf32[0, rows, :] = wconv[k, 0].astype(F32)
            wf32[1, rows, :] = wconv[k, 1].astype(F32)

    for i in range(7):
        gp.last(*ORDER[i])
        project(i)
        gc.last(*ORDER[i])
        gather_rows(*ORDER[i])
    gc.last(*ORDER[7])
    gather_rows(*ORDER[7])

    def to_bf(k, _):
        start = pl.multiple_of(k * CH, CH)
        wbf[0, pl.ds(start, CH), :] = wf32[0, pl.ds(start, CH), :].astype(BF)
        wbf[1, pl.ds(start, CH), :] = wf32[1, pl.ds(start, CH), :].astype(BF)
        return 0

    lax.fori_loop(0, 9, to_bf, 0)
    gp.last(*ORDER[7])
    project(7)

    def flip_weights():
        def step(k, _):
            source = pl.ds(pl.multiple_of(k * CH, CH), CH)
            target = pl.ds(pl.multiple_of((8 - k) * CH, CH), CH)
            wflip[0, target, :] = wf32[0, source, :].T.astype(BF)
            wflip[1, target, :] = wf32[1, source, :].T.astype(BF)
            return 0

        lax.fori_loop(0, 9, step, 0)

    def seg_copy(src, dst, k):
        return pltpu.make_async_remote_copy(
            src_ref=src,
            dst_ref=dst,
            send_sem=seg_s.at[k],
            recv_sem=seg_r.at[k],
            device_id=sibling,
            device_id_type=MESH,
        )

    def halo(e, side, device):
        return pltpu.make_async_remote_copy(
            src_ref=hsend.at[e, side],
            dst_ref=hrecv.at[e, 1 - side],
            send_sem=hs_sem.at[e, side],
            recv_sem=hr_sem.at[e, 1 - side],
            device_id=device,
            device_id_type=MESH,
        )

    def halo_start(e, to_up, to_down):
        halo(e, 0, to_up).start()
        halo(e, 1, to_down).start()

    def halo_sent(e):
        halo(e, 0, up).wait_send()
        halo(e, 1, up).wait_send()

    def halo_here(e):
        halo(e, 0, up).wait_recv()
        halo(e, 1, up).wait_recv()

    def edges(e, source):
        for m in range(MICROS):
            hsend[e, 0, m] = source[m * HALF : m * HALF + 2 * COLS, :]
            hsend[e, 1, m] = source[(m + 1) * HALF - 2 * COLS : (m + 1) * HALF, :]

    def fill(cat, m, row, value):
        a, b, c = shift_parts(value)
        n = value.shape[0] // COLS
        cat[m, row : row + n, :, 0:CH] = a
        cat[m, row : row + n, :, CH : 2 * CH] = b
        cat[m, row : row + n, :, 2 * CH : 3 * CH] = c

    def tokens_of(m):
        return slice(m * HALF, (m + 1) * HALF)

    def conv(weights, which, left):
        total = None
        for ky in range(3):
            value = left(ky)
            value = value.reshape(-1, 3 * CH)
            piece = dot(value, weights[which, ky * 3 * CH : (ky + 1) * 3 * CH, :])
            total = piece if total is None else total + piece
        return total

    def conv_weight_grad(xt, cat, low, which):
        for ky in range(3):
            total = None
            for m in range(MICROS):
                right = cat[m, low - ky : low - ky + ROWS].reshape(HALF, 3 * CH)
                piece = dot(xt[:, tokens_of(m)], right)
                total = piece if total is None else total + piece
            for kx in range(3):
                j = 2 - kx
                row = (3 * ky + kx) * CH
                wf32[which, row : row + CH, :] = total[:, j * CH : (j + 1) * CH]

    def two_convs(cat, weights, first, middle, mid, second, halo_ready):
        for m in range(MICROS):
            v = conv(weights, first, lambda ky: cat[m, 2 + ky : 8 + ky])
            fill(mid, m, 2, middle(m, 1, 6, v))
        halo_ready()
        for low, edge in ((0, 0), (8, 7)):
            v = conv(weights, first, lambda ky: cat[:, low + ky : low + ky + 2])
            for m in range(MICROS):
                u = middle(m, low - 1, 2, v[m * 2 * COLS : (m + 1) * 2 * COLS])
                outer = lax.broadcasted_iota(jnp.int32, u.shape, 0) // COLS == edge // 7
                u = jnp.where(jnp.logical_and(outer, band == edge), 0.0, u)
                fill(mid, m, low, u)
        return [conv(weights, second, lambda ky, m=m: mid[m, ky : ky + ROWS]) for m in range(MICROS)]

    def halo_rows(cat, rows_of):
        for side, row, last in ((0, 0, 0), (1, ROWS + 2, 7)):
            for m in range(MICROS):
                v = rows_of(side, m)
                v = jnp.where(band == last, jnp.zeros_like(v), v)
                fill(cat, m, row, v)

    section_in[...] = acc[...].astype(BF)
    edges(0, section_in)
    halo_start(0, up, down)
    gp.drain()
    gc.drain()

    @pl.when(seg == 1)
    def _():
        flip_weights()
        seg_copy(out, inc, 0).wait_recv()
        section_in[...] = (section_in[...].astype(F32) + inc[...].astype(F32)).astype(BF)

    for m in range(MICROS):
        fill(cat_a, m, 2, gelu(section_in[tokens_of(m), :].astype(F32)).astype(BF).astype(F32))

    def forward_halo():
        halo_here(0)

        @pl.when(seg == 1)
        def _():
            halo_here(1)

        def rows_of(side, m):
            shape = (2 * COLS, CH)
            more = jnp.where(seg == 1, hrecv[1, side, m].astype(F32), 0.0)
            v = (hrecv[0, side, m].astype(F32) + more).astype(BF).astype(F32)
            return gelu(v).astype(BF).astype(F32)

        halo_rows(cat_a, rows_of)

    def keep_hidden(m, row, n, v):
        hidden[m, row + 1 : row + 1 + n] = v.reshape(n, COLS, CH)
        return gelu(v).astype(BF).astype(F32)

    update = two_convs(cat_a, wbf, 0, keep_hidden, cat_b, 1, forward_halo)
    for m in range(MICROS):
        out[tokens_of(m), :] = (section_in[tokens_of(m), :].astype(F32) + update[m]).astype(BF)

    def transposes():
        for m in range(MICROS):
            v = cat_a[m, 2 : 2 + ROWS, :, CH : 2 * CH].reshape(HALF, CH).astype(F32)
            x1t[:, tokens_of(m)] = v.T.astype(BF)
            v = cat_b[m, 1 : 1 + ROWS, :, CH : 2 * CH].reshape(HALF, CH).astype(F32)
            x2t[:, tokens_of(m)] = v.T.astype(BF)

    def sum_copy(k, device):
        return pltpu.make_async_remote_copy(
            src_ref=hsum.at[k],
            dst_ref=hgot.at[k],
            send_sem=sum_s.at[k],
            recv_sem=sum_r.at[k],
            device_id=device,
            device_id_type=MESH,
        )

    rounds = [y1, dp_peer, z1, z2, x1, x2]

    def sum_start(k):
        @pl.when(seg == 1)
        def _():
            sum_copy(k, rounds[k]).start()

    def sum_end(k):
        @pl.when(seg == 1)
        def _():
            sum_copy(k, rounds[k]).wait()
            hsum[k + 1] = hsum[k] + hgot[k]

    @pl.when(seg == 0)
    def _():
        edges(1, out)
        halo_start(1, up_other, down_other)
        to_next = seg_copy(out, inc, 0)
        to_next.start()
        flip_weights()
        transposes()
        to_next.wait_send()
        halo_sent(1)
        seg_copy(grad, og_in, 1).wait_recv()
        og[...] = og_in[...]

    @pl.when(seg == 1)
    def _():
        hw = head_pad[...].astype(BF)
        o = out[...]
        logits = dot(hw, o, ((1,), (1,)))
        albedo = 1.0 / (1.0 + jnp.exp(-logits))
        row = lax.broadcasted_iota(jnp.int32, (8, TOKENS), 0)
        lane = lax.broadcasted_iota(jnp.int32, (8, TOKENS), 1)
        tint = jnp.zeros((8, TOKENS), F32)
        for m in range(MICROS):
            light = illum_ref[m, x]
            for c in range(3):
                tint = jnp.where((row == c) & (lane // HALF == m), light_ref[c, light], tint)
        mismatch = albedo * tint - targets[...]
        lg = (factor * mismatch * tint * albedo * (1.0 - albedo)).astype(BF)
        lgt = lg.astype(F32).T.astype(BF)
        og[...] = dot(lgt, hw).astype(BF)
        edges(2, og)
        halo_start(2, up, down)
        squares = jnp.sum(mismatch * mismatch)
        hg = dot(lg, o)
        row_h = lax.broadcasted_iota(jnp.int32, (8, CH), 0)
        hsum[0] = jnp.where(row_h == 3, squares, hg)

    sum_start(0)

    for m in range(MICROS):
        fill(cat_c, m, 2, og[tokens_of(m), :].astype(F32))

    def backward_halo():
        @pl.when(seg == 1)
        def _():
            halo_here(2)

        @pl.when(seg == 0)
        def _():
            halo_here(3)

        def rows_of(side, m):
            v = jnp.where(seg == 1, hrecv[2, side, m].astype(F32), hrecv[3, side, m].astype(F32))
            return v

        halo_rows(cat_c, rows_of)

    def through(m, row, n, v):
        h = hidden[m, row + 1 : row + 1 + n].reshape(n * COLS, CH)
        return (v * gelu_slope(h)).astype(BF).astype(F32)

    back = two_convs(cat_c, wflip, 1, through, cat_d, 0, backward_halo)
    for m in range(MICROS):
        rows = tokens_of(m)
        slope = gelu_slope(section_in[rows, :].astype(F32))
        grad[rows, :] = (og[rows, :].astype(F32) + back[m] * slope).astype(BF)

    @pl.when(seg == 1)
    def _():
        edges(3, grad)
        halo_start(3, up_other, down_other)
        seg_copy(grad, og_in, 1).start()

    sum_end(0)
    sum_start(1)

    def own_conv(slot, dp, r, dq):
        start = pl.multiple_of(slot * CSLOT, 8)
        return wf32[:, pl.ds(start, CSLOT), :]

    def own_proj(slot, dp, r, dq):
        return part[part_slot(dp, r, dq)]

    def store_conv(v):
        conv_out[...] = v

    def store_proj(v):
        proj_out[...] = v

    rc = Reduce(Axis(False), own_conv, store_conv, wconv, cgot, rcs, rcr)
    rp = Reduce(pa, own_proj, store_proj, wproj, pgot, rps, rpr, placed=True)

    def compute(dp, r):
        xs, ys, _ = pa.coords(dp, r, 0)
        base = xs * 8 + ys * 4
        lanes = pl.ds(pl.multiple_of(base * SLOT, CHUNK), CHUNK)
        v = dot(hooks_v[:, lanes], grad[...], ((0,), (0,)))
        for k in range(4):
            ahead = (k - z + 4) % 4
            block = v[k * SLOT : (k + 1) * SLOT]
            for dq in (0,) + ACROSS:

                @pl.when(ahead == dq % 4)
                def _():
                    if r == 1 and dp in SIDE:
                        wproj[side_slot(dp, dq)] = block.astype(BF)
                    elif dq == 0 or (r == 0 and dp in SIDE):
                        part[part_slot(dp, r, dq)] = block
                    else:
                        wproj[queue_slot(dp, r, dq)] = block.astype(BF)

    for i, (dp, r) in enumerate(BACK):
        compute(dp, r)
        rp.first(dp, r)
        if i == 2:

            @pl.when(seg == 1)
            def _():
                transposes()

            conv_weight_grad(x2t, cat_c, 3, 1)
            conv_weight_grad(x1t, cat_d, 2, 0)
            rc.first(*BACK[0])
            rc.first(*BACK[1])
        if i >= 2:
            rc.first(dp, r)
            if i < 7:
                sum_end(i - 1)
                if i < 6:
                    sum_start(i)
        if i >= 4:
            rc.second(*BACK[i - 2])
            rp.second(*BACK[i - 2])
    final = pltpu.make_async_remote_copy(
        src_ref=hsum.at[6],
        dst_ref=hfin,
        send_sem=seg_s.at[2],
        recv_sem=seg_r.at[2],
        device_id=sibling,
        device_id_type=MESH,
    )

    @pl.when(seg == 1)
    def _():
        final.start()
        total_ref[...] = hsum[6]

    for dp, r in BACK[6:]:
        rc.second(dp, r)
        rp.second(dp, r)
    rc.third()
    rp.third()
    rc.fourth()
    rp.fourth()
    halo_sent(0)

    @pl.when(seg == 1)
    def _():
        halo_sent(2)
        halo_sent(3)
        seg_copy(grad, og_in, 1).wait_send()
        final.wait_send()

    @pl.when(seg == 0)
    def _():
        final.wait_recv()
        total_ref[...] = hfin[...]


def run_main(factor, hooks, proj, conv, head, light, illum, offsets, photos):
    vm = pl.BlockSpec(memory_space=pltpu.VMEM)
    sm = pl.BlockSpec(memory_space=pltpu.SMEM)
    dma = pltpu.SemaphoreType.DMA
    field = pltpu.VMEM((TOKENS, CH), BF)
    return pl.pallas_call(
        functools.partial(main_kernel, factor),
        out_shape=(
            jax.ShapeDtypeStruct((SLOT, CH), F32),
            jax.ShapeDtypeStruct((2, CSLOT, CH), F32),
            jax.ShapeDtypeStruct((8, CH), F32),
        ),
        in_specs=[pl.BlockSpec(memory_space=pl.ANY), vm, vm, vm, sm, sm, sm, pl.BlockSpec(memory_space=pl.ANY)],
        out_specs=(vm, vm, vm),
        scratch_shapes=[
            pltpu.VMEM((TOKENS, D), BF),
            pltpu.VMEM((MICROS, 3, 96, 96), BF),
            pltpu.VMEM((32, SLOT, CH), BF),
            pltpu.VMEM((32, 2, CSLOT, CH), BF),
            pltpu.VMEM((2, 9 * CH, CH), F32),
            pltpu.VMEM((2, 9 * CH, CH), BF),
            pltpu.VMEM((2, 9 * CH, CH), BF),
            pltpu.VMEM((TOKENS, CH), F32),
            field,
            field,
            field,
            field,
            field,
            field,
            pltpu.VMEM((MICROS, ROWS + 2, COLS, CH), F32),
            pltpu.VMEM((MICROS, ROWS + 4, COLS, 3 * CH), BF),
            pltpu.VMEM((MICROS, ROWS + 2, COLS, 3 * CH), BF),
            pltpu.VMEM((MICROS, ROWS + 4, COLS, 3 * CH), BF),
            pltpu.VMEM((MICROS, ROWS + 2, COLS, 3 * CH), BF),
            pltpu.VMEM((CH, TOKENS), BF),
            pltpu.VMEM((CH, TOKENS), BF),
            pltpu.VMEM((4, 2, MICROS, 2 * COLS, CH), BF),
            pltpu.VMEM((4, 2, MICROS, 2 * COLS, CH), BF),
            pltpu.VMEM((8, TOKENS), F32),
            pltpu.VMEM((8, CH), F32),
            pltpu.VMEM((7, 8, CH), F32),
            pltpu.VMEM((6, 8, CH), F32),
            pltpu.VMEM((8, CH), F32),
            pltpu.VMEM((12, SLOT, CH), F32),
            pltpu.VMEM((32, SLOT, CH), BF),
            pltpu.VMEM((32, 2, CSLOT, CH), BF),
            dma((8 + MICROS,)),
            dma((32,)),
            dma((32,)),
            dma((32,)),
            dma((32,)),
            dma((4, 2)),
            dma((4, 2)),
            dma((3,)),
            dma((3,)),
            dma((6,)),
            dma((6,)),
            dma((32,)),
            dma((32,)),
            dma((32,)),
            dma((32,)),
            pltpu.SemaphoreType.REGULAR,
        ],
        compiler_params=pltpu.CompilerParams(
            collective_id=0, has_side_effects=True, vmem_limit_bytes=60 * 1024 * 1024
        ),
        cost_estimate=pl.CostEstimate(
            flops=15_000_000_000, bytes_accessed=14_000_000, transcendentals=1_000_000
        ),
        name="main_kernel",
    )(hooks, proj, conv, head, light, illum, offsets, photos)


def finish_kernel(npix, proj_ref, conv_ref, total_ref, proj_out, conv_out, head_out, loss_out):
    proj_out[...] = proj_ref[...]
    conv_out[...] = conv_ref[...]
    head_out[...] = total_ref[0:3, :]
    loss_out[...] = total_ref[3:4, 0:1] / npix


def run_finish(npix, proj, conv, total):
    vm = pl.BlockSpec(memory_space=pltpu.VMEM)
    return pl.pallas_call(
        functools.partial(finish_kernel, npix),
        out_shape=(
            jax.ShapeDtypeStruct((SLOT, CH), F32),
            jax.ShapeDtypeStruct((2, CSLOT, CH), F32),
            jax.ShapeDtypeStruct((3, CH), F32),
            jax.ShapeDtypeStruct((1, 1), F32),
        ),
        in_specs=[vm, vm, vm],
        out_specs=(vm, vm, vm, vm),
        name="finish_kernel",
    )(proj, conv, total)


def body(hooks, proj_weight, conv_weight, head_weight, light_color, illum, offsets, photos):
    npix = 3 * MICROS * lax.axis_size("dp") * ROWS * lax.axis_size("fsdp") * COLS
    factor = 2.0 * LOSS_SCALE / npix
    tokens = hooks.reshape(TOKENS, D)
    grad_proj, grad_conv, total = run_main(
        factor, tokens, proj_weight[0], conv_weight[0], head_weight, light_color.T,
        illum, offsets.transpose(0, 2, 1), photos,
    )
    grad_proj, grad_conv, head, loss = run_finish(npix, grad_proj, grad_conv, total)
    return (grad_proj[None], grad_conv[None], head, loss[0, 0])


def solution(mesh):
    placed = (
        P("segment", "dp", "fsdp", None, None),
        P("segment", "fsdp", None),
        P("segment", None, "fsdp", None),
        P(),
        P(),
        P("dp", None),
        P("dp", None, None),
        P("dp", None, None, None, None),
    )
    return jax.shard_map(
        body,
        mesh=mesh,
        in_specs=placed,
        out_specs=(P("segment", "fsdp", None), P("segment", None, "fsdp", None), P(), P()),
        check_vma=False,
    )
```

```python
import functools

import jax
import jax.numpy as jnp
from jax import lax
from jax.experimental import pallas as pl
from jax.experimental.pallas import tpu as pltpu
from jax.sharding import PartitionSpec as P

LOSS_SCALE = 8192.0
MESH = pl.DeviceIdType.MESH
BF = jnp.bfloat16
F32 = jnp.float32

MICROS, ROWS, COLS, CH = 2, 8, 64, 256
TOKENS = MICROS * ROWS * COLS
HALF = ROWS * COLS
D = 6144
SLOT = 192
CSLOT = 72
CHUNK = 4 * SLOT

SIDE = (1, -1)
ACROSS = (1, -1, 2)
PLANE = [(1, 0), (-1, 0), (2, 0), (0, 1), (2, 1)]
GREET = PLANE + [(1, 1), (-1, 1)]
ORDER = [(0, 0)] + PLANE + [(1, 1), (-1, 1)]
BACK = [(2, 0), (1, 1), (-1, 1), (2, 1), (1, 0), (-1, 0), (0, 1), (0, 0)]
QUEUE = [BACK[0]] + BACK[3:]


def place():
    f = lax.axis_index("fsdp")
    return f // 8, (f // 4) % 2, f % 4


def at(x, y, z):
    return {"fsdp": x * 8 + y * 4 + z}


def dot(a, b, dims=((1,), (0,))):
    return lax.dot_general(a, b, (dims, ((), ())), preferred_element_type=F32)


def gelu_parts(v):
    c = 0.7978845608028654
    t = jnp.tanh(c * (v + 0.044715 * (v * v * v)))
    return t


def gelu(v):
    return 0.5 * v * (1.0 + gelu_parts(v))


def gelu_slope(v):
    c = 0.7978845608028654
    t = gelu_parts(v)
    return 0.5 * (1.0 + t) + 0.5 * v * (1.0 - t * t) * (c * (1.0 + 3.0 * 0.044715 * (v * v)))


class Axis:
    def __init__(self, p_is_x):
        x, y, z = place()
        self.p_is_x = p_is_x
        self.p, self.y, self.q = (x, y, z) if p_is_x else (z, y, x)

    def coords(self, dp, r, dq):
        p = (self.p + (dp + 4)) % 4
        q = (self.q + (dq + 4)) % 4
        y = (self.y + r) % 2
        return (p, y, q) if self.p_is_x else (q, y, p)

    def slot(self, dp, r, dq):
        x, y, z = self.coords(dp, r, dq)
        return x * 8 + y * 4 + z

    def device(self, dp, r, dq):
        return at(*self.coords(dp, r, dq))

    def fellow(self, dp, r):
        device = self.device(dp, r, 0)
        if (dp, r) == (2, 1):
            device = {"dp": 1 - lax.axis_index("dp"), **device}
        return device

    def beside(self, dp):
        device = self.device(0, 1, 0)
        return device if dp == 1 else {"dp": 1 - lax.axis_index("dp"), **device}


def rel(dp, r, dq):
    return ((dp % 4) * 2 + r) * 4 + dq % 4


class Gather:
    def __init__(self, axis, buf, send, recv):
        self.a, self.buf, self.send, self.recv = axis, buf, send, recv
        self.copies = []

    def put(self, dp, r, dq, to, device=None):
        tp, tr, tq = to
        a = self.a
        slot = a.slot(dp, r, dq)
        copy = pltpu.make_async_remote_copy(
            src_ref=self.buf.at[slot],
            dst_ref=self.buf.at[slot],
            send_sem=self.send.at[len(self.copies)],
            recv_sem=self.recv.at[rel(dp - tp, (r + tr) % 2, dq - tq)],
            device_id=a.device(tp, tr, tq) if device is None else device,
            device_id_type=MESH,
        )
        copy.start()
        self.copies.append(copy)

    def await_(self, dp, r, dq):
        a = self.a
        slot = a.slot(dp, r, dq)
        pltpu.make_async_remote_copy(
            src_ref=self.buf.at[slot],
            dst_ref=self.buf.at[slot],
            send_sem=self.send.at[0],
            recv_sem=self.recv.at[rel(dp, r, dq)],
            device_id=a.device(0, 1, 0),
            device_id_type=MESH,
        ).wait_recv()

    def spread(self):
        for dp, r in PLANE:
            self.put(0, 0, 0, (-dp, r, 0), self.a.fellow(-dp if dp != 2 else 2, r))

    def along(self, dp, r):
        if (dp, r) != (0, 0):
            self.await_(dp, r, 0)
        for dq in ACROSS:
            self.put(dp, r, 0, (0, 0, dq))
        if r == 0 and dp in SIDE:
            self.put(dp, 0, 0, (0, 1, 0), self.a.beside(dp))

    def sideways(self, dq):
        for dp in SIDE:
            self.await_(dp, 0, dq)
            self.put(dp, 0, dq, (0, 1, 0), self.a.beside(dp))

    def last(self, dp, r):
        if r == 1 and dp in SIDE:
            for dq in (0,) + ACROSS:
                self.await_(dp, r, dq)
        elif r == 1 or dp not in SIDE:
            for dq in ACROSS:
                self.await_(dp, r, dq)

    def drain(self):
        for copy in self.copies:
            copy.wait_send()


def entry_barrier(devices):
    barrier = pltpu.get_barrier_semaphore()
    for device in devices:
        pl.semaphore_signal(barrier, inc=1, device_id=device, device_id_type=MESH)
    pl.semaphore_wait(barrier, len(devices))


def partners():
    pa, pc = Axis(True), Axis(False)
    return [pa.device(dp, r, 0) for dp, r in GREET] + [
        pc.device(dp, r, 0) for dp, r in GREET if dp != 0
    ]


def load_rows(source, target, sem):
    copies = []
    for i in range(8):
        rows = pl.ds(i * (TOKENS // 8), TOKENS // 8)
        copy = pltpu.make_async_copy(source.at[rows, :], target.at[rows, :], sem.at[i])
        copy.start()
        copies.append(copy)
    return copies


def shift_parts(v):
    n = v.shape[0]
    grid = (n // COLS, COLS, CH)
    col = lax.broadcasted_iota(jnp.int32, (1, COLS, CH), 1)
    before = jnp.where(col == 0, 0.0, pltpu.roll(v, 1, 0).reshape(grid))
    after = jnp.where(col == COLS - 1, 0.0, pltpu.roll(v, n - 1, 0).reshape(grid))
    return before.astype(BF), v.reshape(grid).astype(BF), after.astype(BF)


class Reduce:
    def __init__(self, axis, own, store, stage, got, send, recv, placed=False):
        self.a = axis
        self.own, self.store = own, store
        self.stage, self.got, self.send, self.recv = stage, got, send, recv
        self.placed = placed
        self.copies = []

    def put(self, k, value, device):
        if value is not None:
            self.stage[k] = value.astype(BF)
        copy = pltpu.make_async_remote_copy(
            src_ref=self.stage.at[k],
            dst_ref=self.got.at[k],
            send_sem=self.send.at[k],
            recv_sem=self.recv.at[k],
            device_id=device,
            device_id_type=MESH,
        )
        copy.start()
        self.copies.append(copy)

    def take(self, k):
        pltpu.make_async_remote_copy(
            src_ref=self.stage.at[k],
            dst_ref=self.got.at[k],
            send_sem=self.send.at[k],
            recv_sem=self.recv.at[k],
            device_id=self.a.device(0, 1, 0),
            device_id_type=MESH,
        ).wait_recv()
        return self.got[k].astype(F32)

    def part(self, dp, r, dq):
        return self.own(self.a.slot(dp, r, dq), dp, r, dq)

    def summed(self, dp, r, dq):
        value = self.part(dp, r, dq)
        if r == 0 and dp in SIDE:
            value = value + self.take(side_slot(dp, dq))
        return value

    def first(self, dp, r):
        if r == 1 and dp in SIDE:
            for dq in ACROSS + (0,):
                value = None if self.placed else self.part(dp, r, dq)
                self.put(side_slot(dp, dq), value, self.a.beside(dp))
        else:
            ready = self.placed and not (r == 0 and dp in SIDE)
            for dq in ACROSS:
                value = None if ready else self.summed(dp, r, dq)
                self.put(queue_slot(dp, r, dq), value, self.a.device(0, 0, dq))

    def second(self, dp, r):
        total = self.summed(dp, r, 0)
        for dq in ACROSS:
            total = total + self.take(queue_slot(dp, r, dq))
        if (dp, r) == (0, 0):
            self.kept = total
        else:
            self.put(26 + PLANE.index((dp, r)), total, self.a.fellow(dp, r))

    def third(self):
        for i in range(len(PLANE)):
            self.kept = self.kept + self.take(26 + i)
        self.put(31, self.kept, {"dp": 1 - lax.axis_index("dp")})

    def fourth(self):
        self.store(self.stage[31].astype(F32) + self.take(31))
        for copy in self.copies:
            copy.wait_send()


def side_slot(dp, dq):
    return SIDE.index(dp) * 4 + dq % 4


def queue_slot(dp, r, dq):
    return 8 + QUEUE.index((dp, r)) * 3 + ACROSS.index(dq)


def part_slot(dp, r, dq):
    if dq == 0:
        return QUEUE.index((dp, r))
    return 6 + SIDE.index(dp) * 3 + ACROSS.index(dq)


def main_kernel(
    factor,
    hooks_ref,
    proj_ref,
    conv_ref,
    head_ref,
    light_ref,
    illum_ref,
    offsets_ref,
    photos_ref,
    proj_out,
    conv_out,
    total_ref,
    hooks_v,
    photos_v,
    wproj,
    wconv,
    wf32,
    wbf,
    wflip,
    acc,
    section_in,
    inc,
    out,
    og_in,
    og,
    grad,
    hidden,
    cat_a,
    cat_b,
    cat_c,
    cat_d,
    x1t,
    x2t,
    hsend,
    hrecv,
    targets,
    head_pad,
    hsum,
    hgot,
    hfin,
    part,
    pgot,
    cgot,
    load_sem,
    psend,
    precv,
    csend,
    crecv,
    hs_sem,
    hr_sem,
    seg_s,
    seg_r,
    sum_s,
    sum_r,
    rps,
    rpr,
    rcs,
    rcr,
    gate,
):
    x, y, z = place()
    seg = lax.axis_index("segment")
    dpi = lax.axis_index("dp")
    band = y * 4 + z
    sibling = {"segment": 1 - seg}
    dp_peer = {"dp": 1 - dpi}
    up_j, down_j = (band + 7) % 8, (band + 1) % 8
    up = at(x, up_j // 4, up_j % 4)
    down = at(x, down_j // 4, down_j % 4)
    up_other = {"segment": 1 - seg, **up}
    down_other = {"segment": 1 - seg, **down}

    pa = Axis(True)
    loads = load_rows(hooks_ref, hooks_v, load_sem)
    pictures = []
    for m in range(MICROS):
        copy = pltpu.make_async_copy(photos_ref.at[m, x], photos_v.at[m], load_sem.at[8 + m])
        copy.start()
        pictures.append(copy)

    me = x * 8 + y * 4 + z
    wproj[me] = proj_ref[...]
    wconv[me] = conv_ref[...]

    z1 = at(x, y, z + 1 - 2 * (z % 2))
    z2 = at(x, y, (z + 2) % 4)
    x1 = at(x + 1 - 2 * (x % 2), y, z)
    x2 = at((x + 2) % 4, y, z)
    y1 = at(x, 1 - y, z)
    entry_barrier(
        partners()
        + [sibling, dp_peer, up_other, down_other, pa.beside(-1)]
        + [pa.fellow(2, 1), Axis(False).fellow(2, 1)]
    )

    gp = Gather(pa, wproj, psend, precv)
    gc = Gather(Axis(False), wconv, csend, crecv)

    @pl.when(seg == 1)
    def _():
        pl.semaphore_wait(gate, 1)

    gp.spread()
    gc.spread()
    gp.along(0, 0)
    gc.along(0, 0)

    yy = lax.broadcasted_iota(jnp.int32, (96, HALF), 0)
    nn = lax.broadcasted_iota(jnp.int32, (96, HALF), 1)
    row8 = lax.broadcasted_iota(jnp.int32, (8, HALF), 0)
    for m in range(MICROS):
        pictures[m].wait()
        oy = offsets_ref[m, 0, x]
        ox = offsets_ref[m, 1, x]
        pick_col = (yy == ox + nn % COLS).astype(F32).astype(BF)
        pick_row = yy == oy + band * ROWS + nn // COLS
        block = jnp.zeros((8, HALF), F32)
        for c in range(3):
            q = dot(photos_v[m, c], pick_col)
            line = jnp.sum(jnp.where(pick_row, q, 0.0), axis=0, keepdims=True)
            block = jnp.where(row8 == c, line, block)
        targets[:, m * HALF : (m + 1) * HALF] = block
    head_pad[...] = jnp.zeros((8, CH), F32)
    head_pad[0:3, :] = head_ref[...].astype(F32)

    acc[...] = jnp.zeros_like(acc)
    for copy in loads:
        copy.wait()

    def project(i):
        dp, r = ORDER[i]
        xs, ys, _ = pa.coords(dp, r, 0)
        base = xs * 8 + ys * 4
        lanes = pl.ds(pl.multiple_of(base * SLOT, CHUNK), CHUNK)
        w = wproj[pl.ds(base, 4)].reshape(CHUNK, CH)

        def step(t, _):
            rows = pl.ds(pl.multiple_of(t * 256, 256), 256)
            acc[rows, :] += dot(hooks_v[rows, lanes], w)
            return 0

        lax.fori_loop(0, TOKENS // 256, step, 0)

    for dp, r in PLANE:
        gp.along(dp, r)
        gc.along(dp, r)
    for dq in ACROSS:
        gp.sideways(dq)
        gc.sideways(dq)

    @pl.when(seg == 0)
    def _():
        pl.semaphore_signal(gate, inc=1, device_id=sibling, device_id_type=MESH)

    pc = gc.a

    def gather_rows(dp, r):
        for dq in (0,) + ACROSS:
            k = pc.slot(dp, r, dq)
            rows = pl.ds(pl.multiple_of(k * CSLOT, 8), CSLOT)
            wf32[0, rows, :] = wconv[k, 0].astype(F32)
            wf32[1, rows, :] = wconv[k, 1].astype(F32)

    for i in range(7):
        gp.last(*ORDER[i])
        project(i)
        gc.last(*ORDER[i])
        gather_rows(*ORDER[i])
    gc.last(*ORDER[7])
    gather_rows(*ORDER[7])

    def to_bf(k, _):
        start = pl.multiple_of(k * CH, CH)
        wbf[0, pl.ds(start, CH), :] = wf32[0, pl.ds(start, CH), :].astype(BF)
        wbf[1, pl.ds(start, CH), :] = wf32[1, pl.ds(start, CH), :].astype(BF)
        return 0

    lax.fori_loop(0, 9, to_bf, 0)
    gp.last(*ORDER[7])
    project(7)

    def flip_weights():
        def step(k, _):
            source = pl.ds(pl.multiple_of(k * CH, CH), CH)
            target = pl.ds(pl.multiple_of((8 - k) * CH, CH), CH)
            wflip[0, target, :] = wf32[0, source, :].T.astype(BF)
            wflip[1, target, :] = wf32[1, source, :].T.astype(BF)
            return 0

        lax.fori_loop(0, 9, step, 0)

    def seg_copy(src, dst, k):
        return pltpu.make_async_remote_copy(
            src_ref=src,
            dst_ref=dst,
            send_sem=seg_s.at[k],
            recv_sem=seg_r.at[k],
            device_id=sibling,
            device_id_type=MESH,
        )

    def halo(e, side, device):
        return pltpu.make_async_remote_copy(
            src_ref=hsend.at[e, side],
            dst_ref=hrecv.at[e, 1 - side],
            send_sem=hs_sem.at[e, side],
            recv_sem=hr_sem.at[e, 1 - side],
            device_id=device,
            device_id_type=MESH,
        )

    def halo_start(e, to_up, to_down):
        halo(e, 0, to_up).start()
        halo(e, 1, to_down).start()

    def halo_sent(e):
        halo(e, 0, up).wait_send()
        halo(e, 1, up).wait_send()

    def halo_here(e):
        halo(e, 0, up).wait_recv()
        halo(e, 1, up).wait_recv()

    def edges(e, source):
        for m in range(MICROS):
            hsend[e, 0, m] = source[m * HALF : m * HALF + 2 * COLS, :]
            hsend[e, 1, m] = source[(m + 1) * HALF - 2 * COLS : (m + 1) * HALF, :]

    def fill(cat, m, row, value):
        a, b, c = shift_parts(value)
        n = value.shape[0] // COLS
        cat[m, row : row + n, :, 0:CH] = a
        cat[m, row : row + n, :, CH : 2 * CH] = b
        cat[m, row : row + n, :, 2 * CH : 3 * CH] = c

    def tokens_of(m):
        return slice(m * HALF, (m + 1) * HALF)

    def conv(weights, which, left):
        total = None
        for ky in range(3):
            value = left(ky)
            value = value.reshape(-1, 3 * CH)
            piece = dot(value, weights[which, ky * 3 * CH : (ky + 1) * 3 * CH, :])
            total = piece if total is None else total + piece
        return total

    def conv_weight_grad(xt, cat, low, which):
        for ky in range(3):
            total = None
            for m in range(MICROS):
                right = cat[m, low - ky : low - ky + ROWS].reshape(HALF, 3 * CH)
                piece = dot(xt[:, tokens_of(m)], right)
                total = piece if total is None else total + piece
            for kx in range(3):
                j = 2 - kx
                row = (3 * ky + kx) * CH
                wf32[which, row : row + CH, :] = total[:, j * CH : (j + 1) * CH]

    def two_convs(cat, weights, first, middle, mid, second, halo_ready):
        for m in range(MICROS):
            v = conv(weights, first, lambda ky: cat[m, 2 + ky : 8 + ky])
            fill(mid, m, 2, middle(m, 1, 6, v))
        halo_ready()
        for low, edge in ((0, 0), (8, 7)):
            v = conv(weights, first, lambda ky: cat[:, low + ky : low + ky + 2])
            for m in range(MICROS):
                u = middle(m, low - 1, 2, v[m * 2 * COLS : (m + 1) * 2 * COLS])
                outer = lax.broadcasted_iota(jnp.int32, u.shape, 0) // COLS == edge // 7
                u = jnp.where(jnp.logical_and(outer, band == edge), 0.0, u)
                fill(mid, m, low, u)
        return [conv(weights, second, lambda ky, m=m: mid[m, ky : ky + ROWS]) for m in range(MICROS)]

    def halo_rows(cat, rows_of):
        for side, row, last in ((0, 0, 0), (1, ROWS + 2, 7)):
            for m in range(MICROS):
                v = rows_of(side, m)
                v = jnp.where(band == last, jnp.zeros_like(v), v)
                fill(cat, m, row, v)

    section_in[...] = acc[...].astype(BF)
    edges(0, section_in)
    halo_start(0, up, down)
    gp.drain()
    gc.drain()

    @pl.when(seg == 1)
    def _():
        flip_weights()
        seg_copy(out, inc, 0).wait_recv()
        section_in[...] = (section_in[...].astype(F32) + inc[...].astype(F32)).astype(BF)

    for m in range(MICROS):
        fill(cat_a, m, 2, gelu(section_in[tokens_of(m), :].astype(F32)).astype(BF).astype(F32))

    def forward_halo():
        halo_here(0)

        @pl.when(seg == 1)
        def _():
            halo_here(1)

        def rows_of(side, m):
            shape = (2 * COLS, CH)
            more = jnp.where(seg == 1, hrecv[1, side, m].astype(F32), 0.0)
            v = (hrecv[0, side, m].astype(F32) + more).astype(BF).astype(F32)
            return gelu(v).astype(BF).astype(F32)

        halo_rows(cat_a, rows_of)

    def keep_hidden(m, row, n, v):
        hidden[m, row + 1 : row + 1 + n] = v.reshape(n, COLS, CH)
        return gelu(v).astype(BF).astype(F32)

    update = two_convs(cat_a, wbf, 0, keep_hidden, cat_b, 1, forward_halo)
    for m in range(MICROS):
        out[tokens_of(m), :] = (section_in[tokens_of(m), :].astype(F32) + update[m]).astype(BF)

    def transposes():
        for m in range(MICROS):
            v = cat_a[m, 2 : 2 + ROWS, :, CH : 2 * CH].reshape(HALF, CH).astype(F32)
            x1t[:, tokens_of(m)] = v.T.astype(BF)
            v = cat_b[m, 1 : 1 + ROWS, :, CH : 2 * CH].reshape(HALF, CH).astype(F32)
            x2t[:, tokens_of(m)] = v.T.astype(BF)

    def sum_copy(k, device):
        return pltpu.make_async_remote_copy(
            src_ref=hsum.at[k],
            dst_ref=hgot.at[k],
            send_sem=sum_s.at[k],
            recv_sem=sum_r.at[k],
            device_id=device,
            device_id_type=MESH,
        )

    rounds = [y1, dp_peer, z1, z2, x1, x2]

    def sum_start(k):
        @pl.when(seg == 1)
        def _():
            sum_copy(k, rounds[k]).start()

    def sum_end(k):
        @pl.when(seg == 1)
        def _():
            sum_copy(k, rounds[k]).wait()
            hsum[k + 1] = hsum[k] + hgot[k]

    @pl.when(seg == 0)
    def _():
        edges(1, out)
        halo_start(1, up_other, down_other)
        to_next = seg_copy(out, inc, 0)
        to_next.start()
        flip_weights()
        transposes()
        to_next.wait_send()
        halo_sent(1)
        seg_copy(grad, og_in, 1).wait_recv()
        og[...] = og_in[...]

    @pl.when(seg == 1)
    def _():
        hw = head_pad[...].astype(BF)
        o = out[...]
        logits = dot(hw, o, ((1,), (1,)))
        albedo = 1.0 / (1.0 + jnp.exp(-logits))
        row = lax.broadcasted_iota(jnp.int32, (8, TOKENS), 0)
        lane = lax.broadcasted_iota(jnp.int32, (8, TOKENS), 1)
        tint = jnp.zeros((8, TOKENS), F32)
        for m in range(MICROS):
            light = illum_ref[m, x]
            for c in range(3):
                tint = jnp.where((row == c) & (lane // HALF == m), light_ref[c, light], tint)
        mismatch = albedo * tint - targets[...]
        lg = (factor * mismatch * tint * albedo * (1.0 - albedo)).astype(BF)
        lgt = lg.astype(F32).T.astype(BF)
        og[...] = dot(lgt, hw).astype(BF)
        edges(2, og)
        halo_start(2, up, down)
        squares = jnp.sum(mismatch * mismatch)
        hg = dot(lg, o)
        row_h = lax.broadcasted_iota(jnp.int32, (8, CH), 0)
        hsum[0] = jnp.where(row_h == 3, squares, hg)

    sum_start(0)

    for m in range(MICROS):
        fill(cat_c, m, 2, og[tokens_of(m), :].astype(F32))

    def backward_halo():
        @pl.when(seg == 1)
        def _():
            halo_here(2)

        @pl.when(seg == 0)
        def _():
            halo_here(3)

        def rows_of(side, m):
            v = jnp.where(seg == 1, hrecv[2, side, m].astype(F32), hrecv[3, side, m].astype(F32))
            return v

        halo_rows(cat_c, rows_of)

    def through(m, row, n, v):
        h = hidden[m, row + 1 : row + 1 + n].reshape(n * COLS, CH)
        return (v * gelu_slope(h)).astype(BF).astype(F32)

    back = two_convs(cat_c, wflip, 1, through, cat_d, 0, backward_halo)
    for m in range(MICROS):
        rows = tokens_of(m)
        slope = gelu_slope(section_in[rows, :].astype(F32))
        grad[rows, :] = (og[rows, :].astype(F32) + back[m] * slope).astype(BF)

    @pl.when(seg == 1)
    def _():
        edges(3, grad)
        halo_start(3, up_other, down_other)
        seg_copy(grad, og_in, 1).start()

    sum_end(0)
    sum_start(1)

    def own_conv(slot, dp, r, dq):
        start = pl.multiple_of(slot * CSLOT, 8)
        return wf32[:, pl.ds(start, CSLOT), :]

    def own_proj(slot, dp, r, dq):
        return part[part_slot(dp, r, dq)]

    def store_conv(v):
        conv_out[...] = v

    def store_proj(v):
        proj_out[...] = v

    rc = Reduce(Axis(False), own_conv, store_conv, wconv, cgot, rcs, rcr)
    rp = Reduce(pa, own_proj, store_proj, wproj, pgot, rps, rpr, placed=True)

    def compute(dp, r):
        xs, ys, _ = pa.coords(dp, r, 0)
        base = xs * 8 + ys * 4
        lanes = pl.ds(pl.multiple_of(base * SLOT, CHUNK), CHUNK)
        v = dot(hooks_v[:, lanes], grad[...], ((0,), (0,)))
        for k in range(4):
            ahead = (k - z + 4) % 4
            block = v[k * SLOT : (k + 1) * SLOT]
            for dq in (0,) + ACROSS:

                @pl.when(ahead == dq % 4)
                def _():
                    if r == 1 and dp in SIDE:
                        wproj[side_slot(dp, dq)] = block.astype(BF)
                    elif dq == 0 or (r == 0 and dp in SIDE):
                        part[part_slot(dp, r, dq)] = block
                    else:
                        wproj[queue_slot(dp, r, dq)] = block.astype(BF)

    for i, (dp, r) in enumerate(BACK):
        compute(dp, r)
        rp.first(dp, r)
        if i == 2:

            @pl.when(seg == 1)
            def _():
                transposes()

            conv_weight_grad(x2t, cat_c, 3, 1)
            conv_weight_grad(x1t, cat_d, 2, 0)
            rc.first(*BACK[0])
            rc.first(*BACK[1])
        if i >= 2:
            rc.first(dp, r)
            if i < 7:
                sum_end(i - 1)
                if i < 6:
                    sum_start(i)
        if i >= 5:
            rc.second(*QUEUE[i - 5])
            rp.second(*QUEUE[i - 5])
    final = pltpu.make_async_remote_copy(
        src_ref=hsum.at[6],
        dst_ref=hfin,
        send_sem=seg_s.at[2],
        recv_sem=seg_r.at[2],
        device_id=sibling,
        device_id_type=MESH,
    )

    @pl.when(seg == 1)
    def _():
        final.start()
        total_ref[...] = hsum[6]

    for dp, r in QUEUE[3:]:
        rc.second(dp, r)
        rp.second(dp, r)
    rc.third()
    rp.third()
    rc.fourth()
    rp.fourth()
    halo_sent(0)

    @pl.when(seg == 1)
    def _():
        halo_sent(2)
        halo_sent(3)
        seg_copy(grad, og_in, 1).wait_send()
        final.wait_send()

    @pl.when(seg == 0)
    def _():
        final.wait_recv()
        total_ref[...] = hfin[...]


def run_main(factor, hooks, proj, conv, head, light, illum, offsets, photos):
    vm = pl.BlockSpec(memory_space=pltpu.VMEM)
    sm = pl.BlockSpec(memory_space=pltpu.SMEM)
    dma = pltpu.SemaphoreType.DMA
    field = pltpu.VMEM((TOKENS, CH), BF)
    return pl.pallas_call(
        functools.partial(main_kernel, factor),
        out_shape=(
            jax.ShapeDtypeStruct((SLOT, CH), F32),
            jax.ShapeDtypeStruct((2, CSLOT, CH), F32),
            jax.ShapeDtypeStruct((8, CH), F32),
        ),
        in_specs=[pl.BlockSpec(memory_space=pl.ANY), vm, vm, vm, sm, sm, sm, pl.BlockSpec(memory_space=pl.ANY)],
        out_specs=(vm, vm, vm),
        scratch_shapes=[
            pltpu.VMEM((TOKENS, D), BF),
            pltpu.VMEM((MICROS, 3, 96, 96), BF),
            pltpu.VMEM((32, SLOT, CH), BF),
            pltpu.VMEM((32, 2, CSLOT, CH), BF),
            pltpu.VMEM((2, 9 * CH, CH), F32),
            pltpu.VMEM((2, 9 * CH, CH), BF),
            pltpu.VMEM((2, 9 * CH, CH), BF),
            pltpu.VMEM((TOKENS, CH), F32),
            field,
            field,
            field,
            field,
            field,
            field,
            pltpu.VMEM((MICROS, ROWS + 2, COLS, CH), F32),
            pltpu.VMEM((MICROS, ROWS + 4, COLS, 3 * CH), BF),
            pltpu.VMEM((MICROS, ROWS + 2, COLS, 3 * CH), BF),
            pltpu.VMEM((MICROS, ROWS + 4, COLS, 3 * CH), BF),
            pltpu.VMEM((MICROS, ROWS + 2, COLS, 3 * CH), BF),
            pltpu.VMEM((CH, TOKENS), BF),
            pltpu.VMEM((CH, TOKENS), BF),
            pltpu.VMEM((4, 2, MICROS, 2 * COLS, CH), BF),
            pltpu.VMEM((4, 2, MICROS, 2 * COLS, CH), BF),
            pltpu.VMEM((8, TOKENS), F32),
            pltpu.VMEM((8, CH), F32),
            pltpu.VMEM((7, 8, CH), F32),
            pltpu.VMEM((6, 8, CH), F32),
            pltpu.VMEM((8, CH), F32),
            pltpu.VMEM((12, SLOT, CH), F32),
            pltpu.VMEM((32, SLOT, CH), BF),
            pltpu.VMEM((32, 2, CSLOT, CH), BF),
            dma((8 + MICROS,)),
            dma((32,)),
            dma((32,)),
            dma((32,)),
            dma((32,)),
            dma((4, 2)),
            dma((4, 2)),
            dma((3,)),
            dma((3,)),
            dma((6,)),
            dma((6,)),
            dma((32,)),
            dma((32,)),
            dma((32,)),
            dma((32,)),
            pltpu.SemaphoreType.REGULAR,
        ],
        compiler_params=pltpu.CompilerParams(
            collective_id=0, has_side_effects=True, vmem_limit_bytes=60 * 1024 * 1024
        ),
        cost_estimate=pl.CostEstimate(
            flops=15_000_000_000, bytes_accessed=14_000_000, transcendentals=1_000_000
        ),
        name="main_kernel",
    )(hooks, proj, conv, head, light, illum, offsets, photos)


def finish_kernel(npix, proj_ref, conv_ref, total_ref, proj_out, conv_out, head_out, loss_out):
    proj_out[...] = proj_ref[...]
    conv_out[...] = conv_ref[...]
    head_out[...] = total_ref[0:3, :]
    loss_out[...] = total_ref[3:4, 0:1] / npix


def run_finish(npix, proj, conv, total):
    vm = pl.BlockSpec(memory_space=pltpu.VMEM)
    return pl.pallas_call(
        functools.partial(finish_kernel, npix),
        out_shape=(
            jax.ShapeDtypeStruct((SLOT, CH), F32),
            jax.ShapeDtypeStruct((2, CSLOT, CH), F32),
            jax.ShapeDtypeStruct((3, CH), F32),
            jax.ShapeDtypeStruct((1, 1), F32),
        ),
        in_specs=[vm, vm, vm],
        out_specs=(vm, vm, vm, vm),
        name="finish_kernel",
    )(proj, conv, total)


def body(hooks, proj_weight, conv_weight, head_weight, light_color, illum, offsets, photos):
    npix = 3 * MICROS * lax.axis_size("dp") * ROWS * lax.axis_size("fsdp") * COLS
    factor = 2.0 * LOSS_SCALE / npix
    tokens = hooks.reshape(TOKENS, D)
    grad_proj, grad_conv, total = run_main(
        factor, tokens, proj_weight[0], conv_weight[0], head_weight, light_color.T,
        illum, offsets.transpose(0, 2, 1), photos,
    )
    grad_proj, grad_conv, head, loss = run_finish(npix, grad_proj, grad_conv, total)
    return (grad_proj[None], grad_conv[None], head, loss[0, 0])


def solution(mesh):
    placed = (
        P("segment", "dp", "fsdp", None, None),
        P("segment", "fsdp", None),
        P("segment", None, "fsdp", None),
        P(),
        P(),
        P("dp", None),
        P("dp", None, None),
        P("dp", None, None, None, None),
    )
    return jax.shard_map(
        body,
        mesh=mesh,
        in_specs=placed,
        out_specs=(P("segment", "fsdp", None), P("segment", None, "fsdp", None), P(), P()),
        check_vma=False,
    )
```

```python
import functools

import jax
import jax.numpy as jnp
from jax import lax
from jax.experimental import pallas as pl
from jax.experimental.pallas import tpu as pltpu
from jax.sharding import PartitionSpec as P

LOSS_SCALE = 8192.0
MESH = pl.DeviceIdType.MESH
BF = jnp.bfloat16
F32 = jnp.float32

MICROS, ROWS, COLS, CH = 2, 8, 64, 256
TOKENS = MICROS * ROWS * COLS
HALF = ROWS * COLS
D = 6144
SLOT = 192
CSLOT = 72
CHUNK = 4 * SLOT

SIDE = (1, -1)
ACROSS = (2, 1, -1)
PLANE = [(1, 0), (-1, 0), (2, 0), (0, 1), (2, 1)]
GREET = PLANE + [(1, 1), (-1, 1)]
ORDER = [(0, 0)] + PLANE + [(1, 1), (-1, 1)]
BACK = [(2, 0), (1, 1), (-1, 1), (2, 1), (1, 0), (-1, 0), (0, 1), (0, 0)]
QUEUE = [BACK[0]] + BACK[3:]


def place():
    f = lax.axis_index("fsdp")
    return f // 8, (f // 4) % 2, f % 4


def at(x, y, z):
    return {"fsdp": x * 8 + y * 4 + z}


def dot(a, b, dims=((1,), (0,))):
    return lax.dot_general(a, b, (dims, ((), ())), preferred_element_type=F32)


def gelu_parts(v):
    c = 0.7978845608028654
    t = jnp.tanh(c * (v + 0.044715 * (v * v * v)))
    return t


def gelu(v):
    return 0.5 * v * (1.0 + gelu_parts(v))


def gelu_slope(v):
    c = 0.7978845608028654
    t = gelu_parts(v)
    return 0.5 * (1.0 + t) + 0.5 * v * (1.0 - t * t) * (c * (1.0 + 3.0 * 0.044715 * (v * v)))


class Axis:
    def __init__(self, p_is_x):
        x, y, z = place()
        self.p_is_x = p_is_x
        self.p, self.y, self.q = (x, y, z) if p_is_x else (z, y, x)

    def coords(self, dp, r, dq):
        p = (self.p + (dp + 4)) % 4
        q = (self.q + (dq + 4)) % 4
        y = (self.y + r) % 2
        return (p, y, q) if self.p_is_x else (q, y, p)

    def slot(self, dp, r, dq):
        x, y, z = self.coords(dp, r, dq)
        return x * 8 + y * 4 + z

    def device(self, dp, r, dq):
        return at(*self.coords(dp, r, dq))

    def fellow(self, dp, r):
        device = self.device(dp, r, 0)
        if (dp, r) == (2, 1):
            device = {"dp": 1 - lax.axis_index("dp"), **device}
        return device

    def beside(self, dp):
        device = self.device(0, 1, 0)
        return device if dp == 1 else {"dp": 1 - lax.axis_index("dp"), **device}


def rel(dp, r, dq):
    return ((dp % 4) * 2 + r) * 4 + dq % 4


class Gather:
    def __init__(self, axis, buf, send, recv):
        self.a, self.buf, self.send, self.recv = axis, buf, send, recv
        self.copies = []

    def put(self, dp, r, dq, to, device=None):
        tp, tr, tq = to
        a = self.a
        slot = a.slot(dp, r, dq)
        copy = pltpu.make_async_remote_copy(
            src_ref=self.buf.at[slot],
            dst_ref=self.buf.at[slot],
            send_sem=self.send.at[len(self.copies)],
            recv_sem=self.recv.at[rel(dp - tp, (r + tr) % 2, dq - tq)],
            device_id=a.device(tp, tr, tq) if device is None else device,
            device_id_type=MESH,
        )
        copy.start()
        self.copies.append(copy)

    def await_(self, dp, r, dq):
        a = self.a
        slot = a.slot(dp, r, dq)
        pltpu.make_async_remote_copy(
            src_ref=self.buf.at[slot],
            dst_ref=self.buf.at[slot],
            send_sem=self.send.at[0],
            recv_sem=self.recv.at[rel(dp, r, dq)],
            device_id=a.device(0, 1, 0),
            device_id_type=MESH,
        ).wait_recv()

    def spread(self):
        for dp, r in PLANE:
            self.put(0, 0, 0, (-dp, r, 0), self.a.fellow(-dp if dp != 2 else 2, r))

    def along(self, dp, r):
        if (dp, r) != (0, 0):
            self.await_(dp, r, 0)
        for dq in ACROSS:
            self.put(dp, r, 0, (0, 0, dq))
        if r == 0 and dp in SIDE:
            self.put(dp, 0, 0, (0, 1, 0), self.a.beside(dp))

    def sideways(self, dq):
        for dp in SIDE:
            self.await_(dp, 0, dq)
            self.put(dp, 0, dq, (0, 1, 0), self.a.beside(dp))

    def last(self, dp, r):
        if r == 1 and dp in SIDE:
            for dq in (0,) + ACROSS:
                self.await_(dp, r, dq)
        elif r == 1 or dp not in SIDE:
            for dq in ACROSS:
                self.await_(dp, r, dq)

    def drain(self):
        for copy in self.copies:
            copy.wait_send()


def entry_barrier(devices):
    barrier = pltpu.get_barrier_semaphore()
    for device in devices:
        pl.semaphore_signal(barrier, inc=1, device_id=device, device_id_type=MESH)
    pl.semaphore_wait(barrier, len(devices))


def partners():
    pa, pc = Axis(True), Axis(False)
    return [pa.device(dp, r, 0) for dp, r in GREET] + [
        pc.device(dp, r, 0) for dp, r in GREET if dp != 0
    ]


def load_rows(source, target, sem):
    copies = []
    for i in range(8):
        rows = pl.ds(i * (TOKENS // 8), TOKENS // 8)
        copy = pltpu.make_async_copy(source.at[rows, :], target.at[rows, :], sem.at[i])
        copy.start()
        copies.append(copy)
    return copies


def shift_parts(v):
    n = v.shape[0]
    grid = (n // COLS, COLS, CH)
    col = lax.broadcasted_iota(jnp.int32, (1, COLS, CH), 1)
    before = jnp.where(col == 0, 0.0, pltpu.roll(v, 1, 0).reshape(grid))
    after = jnp.where(col == COLS - 1, 0.0, pltpu.roll(v, n - 1, 0).reshape(grid))
    return before.astype(BF), v.reshape(grid).astype(BF), after.astype(BF)


class Reduce:
    def __init__(self, axis, own, store, stage, got, send, recv, placed=False):
        self.a = axis
        self.own, self.store = own, store
        self.stage, self.got, self.send, self.recv = stage, got, send, recv
        self.placed = placed
        self.copies = []

    def put(self, k, value, device):
        if value is not None:
            self.stage[k] = value.astype(BF)
        copy = pltpu.make_async_remote_copy(
            src_ref=self.stage.at[k],
            dst_ref=self.got.at[k],
            send_sem=self.send.at[k],
            recv_sem=self.recv.at[k],
            device_id=device,
            device_id_type=MESH,
        )
        copy.start()
        self.copies.append(copy)

    def take(self, k):
        pltpu.make_async_remote_copy(
            src_ref=self.stage.at[k],
            dst_ref=self.got.at[k],
            send_sem=self.send.at[k],
            recv_sem=self.recv.at[k],
            device_id=self.a.device(0, 1, 0),
            device_id_type=MESH,
        ).wait_recv()
        return self.got[k].astype(F32)

    def part(self, dp, r, dq):
        return self.own(self.a.slot(dp, r, dq), dp, r, dq)

    def summed(self, dp, r, dq):
        value = self.part(dp, r, dq)
        if r == 0 and dp in SIDE:
            value = value + self.take(side_slot(dp, dq))
        return value

    def first(self, dp, r):
        if r == 1 and dp in SIDE:
            for dq in ACROSS + (0,):
                value = None if self.placed else self.part(dp, r, dq)
                self.put(side_slot(dp, dq), value, self.a.beside(dp))
        else:
            ready = self.placed and not (r == 0 and dp in SIDE)
            for dq in ACROSS:
                value = None if ready else self.summed(dp, r, dq)
                self.put(queue_slot(dp, r, dq), value, self.a.device(0, 0, dq))

    def second(self, dp, r):
        total = self.summed(dp, r, 0)
        for dq in ACROSS:
            total = total + self.take(queue_slot(dp, r, dq))
        if (dp, r) == (0, 0):
            self.kept = total
        else:
            self.put(26 + PLANE.index((dp, r)), total, self.a.fellow(dp, r))

    def third(self):
        for i in range(len(PLANE)):
            self.kept = self.kept + self.take(26 + i)
        self.put(31, self.kept, {"dp": 1 - lax.axis_index("dp")})

    def fourth(self):
        self.store(self.stage[31].astype(F32) + self.take(31))
        for copy in self.copies:
            copy.wait_send()


def side_slot(dp, dq):
    return SIDE.index(dp) * 4 + dq % 4


def queue_slot(dp, r, dq):
    return 8 + QUEUE.index((dp, r)) * 3 + ACROSS.index(dq)


def part_slot(dp, r, dq):
    if dq == 0:
        return QUEUE.index((dp, r))
    return 6 + SIDE.index(dp) * 3 + ACROSS.index(dq)


def main_kernel(
    factor,
    hooks_ref,
    proj_ref,
    conv_ref,
    head_ref,
    light_ref,
    illum_ref,
    offsets_ref,
    photos_ref,
    proj_out,
    conv_out,
    total_ref,
    hooks_v,
    photos_v,
    wproj,
    wconv,
    wf32,
    wbf,
    wflip,
    acc,
    section_in,
    inc,
    out,
    og_in,
    og,
    grad,
    hidden,
    cat_a,
    cat_b,
    cat_c,
    cat_d,
    x1t,
    x2t,
    hsend,
    hrecv,
    targets,
    head_pad,
    hsum,
    hgot,
    hfin,
    part,
    pgot,
    cgot,
    load_sem,
    psend,
    precv,
    csend,
    crecv,
    hs_sem,
    hr_sem,
    seg_s,
    seg_r,
    sum_s,
    sum_r,
    rps,
    rpr,
    rcs,
    rcr,
    gate,
):
    x, y, z = place()
    seg = lax.axis_index("segment")
    dpi = lax.axis_index("dp")
    band = y * 4 + z
    sibling = {"segment": 1 - seg}
    dp_peer = {"dp": 1 - dpi}
    up_j, down_j = (band + 7) % 8, (band + 1) % 8
    up = at(x, up_j // 4, up_j % 4)
    down = at(x, down_j // 4, down_j % 4)
    up_other = {"segment": 1 - seg, **up}
    down_other = {"segment": 1 - seg, **down}

    pa = Axis(True)
    loads = load_rows(hooks_ref, hooks_v, load_sem)
    pictures = []
    for m in range(MICROS):
        copy = pltpu.make_async_copy(photos_ref.at[m, x], photos_v.at[m], load_sem.at[8 + m])
        copy.start()
        pictures.append(copy)

    me = x * 8 + y * 4 + z
    wproj[me] = proj_ref[...]
    wconv[me] = conv_ref[...]

    z1 = at(x, y, z + 1 - 2 * (z % 2))
    z2 = at(x, y, (z + 2) % 4)
    x1 = at(x + 1 - 2 * (x % 2), y, z)
    x2 = at((x + 2) % 4, y, z)
    y1 = at(x, 1 - y, z)
    entry_barrier(
        partners()
        + [sibling, dp_peer, up_other, down_other, pa.beside(-1)]
        + [pa.fellow(2, 1), Axis(False).fellow(2, 1)]
    )

    gp = Gather(pa, wproj, psend, precv)
    gc = Gather(Axis(False), wconv, csend, crecv)

    @pl.when(seg == 1)
    def _():
        pl.semaphore_wait(gate, 1)

    gp.spread()
    gc.spread()
    gp.along(0, 0)
    gc.along(0, 0)

    yy = lax.broadcasted_iota(jnp.int32, (96, HALF), 0)
    nn = lax.broadcasted_iota(jnp.int32, (96, HALF), 1)
    row8 = lax.broadcasted_iota(jnp.int32, (8, HALF), 0)
    for m in range(MICROS):
        pictures[m].wait()
        oy = offsets_ref[m, 0, x]
        ox = offsets_ref[m, 1, x]
        pick_col = (yy == ox + nn % COLS).astype(F32).astype(BF)
        pick_row = yy == oy + band * ROWS + nn // COLS
        block = jnp.zeros((8, HALF), F32)
        for c in range(3):
            q = dot(photos_v[m, c], pick_col)
            line = jnp.sum(jnp.where(pick_row, q, 0.0), axis=0, keepdims=True)
            block = jnp.where(row8 == c, line, block)
        targets[:, m * HALF : (m + 1) * HALF] = block
    head_pad[...] = jnp.zeros((8, CH), F32)
    head_pad[0:3, :] = head_ref[...].astype(F32)

    acc[...] = jnp.zeros_like(acc)
    for copy in loads:
        copy.wait()

    def project(i):
        dp, r = ORDER[i]
        xs, ys, _ = pa.coords(dp, r, 0)
        base = xs * 8 + ys * 4
        lanes = pl.ds(pl.multiple_of(base * SLOT, CHUNK), CHUNK)
        w = wproj[pl.ds(base, 4)].reshape(CHUNK, CH)

        def step(t, _):
            rows = pl.ds(pl.multiple_of(t * 256, 256), 256)
            acc[rows, :] += dot(hooks_v[rows, lanes], w)
            return 0

        lax.fori_loop(0, TOKENS // 256, step, 0)

    for dp, r in PLANE:
        gp.along(dp, r)
        gc.along(dp, r)
    for dq in (1, -1, 2):
        gp.sideways(dq)
        gc.sideways(dq)

    @pl.when(seg == 0)
    def _():
        pl.semaphore_signal(gate, inc=1, device_id=sibling, device_id_type=MESH)

    pc = gc.a

    def gather_rows(dp, r):
        for dq in (0,) + ACROSS:
            k = pc.slot(dp, r, dq)
            rows = pl.ds(pl.multiple_of(k * CSLOT, 8), CSLOT)
            wf32[0, rows, :] = wconv[k, 0].astype(F32)
            wf32[1, rows, :] = wconv[k, 1].astype(F32)

    for i in range(7):
        gp.last(*ORDER[i])
        project(i)
        gc.last(*ORDER[i])
        gather_rows(*ORDER[i])
    gc.last(*ORDER[7])
    gather_rows(*ORDER[7])

    def to_bf(k, _):
        start = pl.multiple_of(k * CH, CH)
        wbf[0, pl.ds(start, CH), :] = wf32[0, pl.ds(start, CH), :].astype(BF)
        wbf[1, pl.ds(start, CH), :] = wf32[1, pl.ds(start, CH), :].astype(BF)
        return 0

    lax.fori_loop(0, 9, to_bf, 0)
    gp.last(*ORDER[7])
    project(7)

    def flip_weights():
        def step(k, _):
            source = pl.ds(pl.multiple_of(k * CH, CH), CH)
            target = pl.ds(pl.multiple_of((8 - k) * CH, CH), CH)
            wflip[0, target, :] = wf32[0, source, :].T.astype(BF)
            wflip[1, target, :] = wf32[1, source, :].T.astype(BF)
            return 0

        lax.fori_loop(0, 9, step, 0)

    def seg_copy(src, dst, k):
        return pltpu.make_async_remote_copy(
            src_ref=src,
            dst_ref=dst,
            send_sem=seg_s.at[k],
            recv_sem=seg_r.at[k],
            device_id=sibling,
            device_id_type=MESH,
        )

    def halo(e, side, device):
        return pltpu.make_async_remote_copy(
            src_ref=hsend.at[e, side],
            dst_ref=hrecv.at[e, 1 - side],
            send_sem=hs_sem.at[e, side],
            recv_sem=hr_sem.at[e, 1 - side],
            device_id=device,
            device_id_type=MESH,
        )

    def halo_start(e, to_up, to_down):
        halo(e, 0, to_up).start()
        halo(e, 1, to_down).start()

    def halo_sent(e):
        halo(e, 0, up).wait_send()
        halo(e, 1, up).wait_send()

    def halo_here(e):
        halo(e, 0, up).wait_recv()
        halo(e, 1, up).wait_recv()

    def edges(e, source):
        for m in range(MICROS):
            hsend[e, 0, m] = source[m * HALF : m * HALF + 2 * COLS, :]
            hsend[e, 1, m] = source[(m + 1) * HALF - 2 * COLS : (m + 1) * HALF, :]

    def fill(cat, m, row, value):
        a, b, c = shift_parts(value)
        n = value.shape[0] // COLS
        cat[m, row : row + n, :, 0:CH] = a
        cat[m, row : row + n, :, CH : 2 * CH] = b
        cat[m, row : row + n, :, 2 * CH : 3 * CH] = c

    def tokens_of(m):
        return slice(m * HALF, (m + 1) * HALF)

    def conv(weights, which, left):
        total = None
        for ky in range(3):
            value = left(ky)
            value = value.reshape(-1, 3 * CH)
            piece = dot(value, weights[which, ky * 3 * CH : (ky + 1) * 3 * CH, :])
            total = piece if total is None else total + piece
        return total

    def conv_weight_grad(xt, cat, low, which):
        for ky in range(3):
            total = None
            for m in range(MICROS):
                right = cat[m, low - ky : low - ky + ROWS].reshape(HALF, 3 * CH)
                piece = dot(xt[:, tokens_of(m)], right)
                total = piece if total is None else total + piece
            for kx in range(3):
                j = 2 - kx
                row = (3 * ky + kx) * CH
                wf32[which, row : row + CH, :] = total[:, j * CH : (j + 1) * CH]

    def two_convs(cat, weights, first, middle, mid, second, halo_ready):
        for m in range(MICROS):
            v = conv(weights, first, lambda ky: cat[m, 2 + ky : 8 + ky])
            fill(mid, m, 2, middle(m, 1, 6, v))
        halo_ready()
        for low, edge in ((0, 0), (8, 7)):
            v = conv(weights, first, lambda ky: cat[:, low + ky : low + ky + 2])
            for m in range(MICROS):
                u = middle(m, low - 1, 2, v[m * 2 * COLS : (m + 1) * 2 * COLS])
                outer = lax.broadcasted_iota(jnp.int32, u.shape, 0) // COLS == edge // 7
                u = jnp.where(jnp.logical_and(outer, band == edge), 0.0, u)
                fill(mid, m, low, u)
        return [conv(weights, second, lambda ky, m=m: mid[m, ky : ky + ROWS]) for m in range(MICROS)]

    def halo_rows(cat, rows_of):
        for side, row, last in ((0, 0, 0), (1, ROWS + 2, 7)):
            for m in range(MICROS):
                v = rows_of(side, m)
                v = jnp.where(band == last, jnp.zeros_like(v), v)
                fill(cat, m, row, v)

    section_in[...] = acc[...].astype(BF)
    edges(0, section_in)
    halo_start(0, up, down)
    gp.drain()
    gc.drain()

    @pl.when(seg == 1)
    def _():
        flip_weights()
        seg_copy(out, inc, 0).wait_recv()
        section_in[...] = (section_in[...].astype(F32) + inc[...].astype(F32)).astype(BF)

    for m in range(MICROS):
        fill(cat_a, m, 2, gelu(section_in[tokens_of(m), :].astype(F32)).astype(BF).astype(F32))

    def forward_halo():
        halo_here(0)

        @pl.when(seg == 1)
        def _():
            halo_here(1)

        def rows_of(side, m):
            shape = (2 * COLS, CH)
            more = jnp.where(seg == 1, hrecv[1, side, m].astype(F32), 0.0)
            v = (hrecv[0, side, m].astype(F32) + more).astype(BF).astype(F32)
            return gelu(v).astype(BF).astype(F32)

        halo_rows(cat_a, rows_of)

    def keep_hidden(m, row, n, v):
        hidden[m, row + 1 : row + 1 + n] = v.reshape(n, COLS, CH)
        return gelu(v).astype(BF).astype(F32)

    update = two_convs(cat_a, wbf, 0, keep_hidden, cat_b, 1, forward_halo)
    for m in range(MICROS):
        out[tokens_of(m), :] = (section_in[tokens_of(m), :].astype(F32) + update[m]).astype(BF)

    def transposes():
        for m in range(MICROS):
            v = cat_a[m, 2 : 2 + ROWS, :, CH : 2 * CH].reshape(HALF, CH).astype(F32)
            x1t[:, tokens_of(m)] = v.T.astype(BF)
            v = cat_b[m, 1 : 1 + ROWS, :, CH : 2 * CH].reshape(HALF, CH).astype(F32)
            x2t[:, tokens_of(m)] = v.T.astype(BF)

    def sum_copy(k, device):
        return pltpu.make_async_remote_copy(
            src_ref=hsum.at[k],
            dst_ref=hgot.at[k],
            send_sem=sum_s.at[k],
            recv_sem=sum_r.at[k],
            device_id=device,
            device_id_type=MESH,
        )

    rounds = [y1, dp_peer, z1, z2, x1, x2]

    def sum_start(k):
        @pl.when(seg == 1)
        def _():
            sum_copy(k, rounds[k]).start()

    def sum_end(k):
        @pl.when(seg == 1)
        def _():
            sum_copy(k, rounds[k]).wait()
            hsum[k + 1] = hsum[k] + hgot[k]

    @pl.when(seg == 0)
    def _():
        edges(1, out)
        halo_start(1, up_other, down_other)
        to_next = seg_copy(out, inc, 0)
        to_next.start()
        flip_weights()
        transposes()
        to_next.wait_send()
        halo_sent(1)
        seg_copy(grad, og_in, 1).wait_recv()
        og[...] = og_in[...]

    @pl.when(seg == 1)
    def _():
        hw = head_pad[...].astype(BF)
        o = out[...]
        logits = dot(hw, o, ((1,), (1,)))
        albedo = 1.0 / (1.0 + jnp.exp(-logits))
        row = lax.broadcasted_iota(jnp.int32, (8, TOKENS), 0)
        lane = lax.broadcasted_iota(jnp.int32, (8, TOKENS), 1)
        tint = jnp.zeros((8, TOKENS), F32)
        for m in range(MICROS):
            light = illum_ref[m, x]
            for c in range(3):
                tint = jnp.where((row == c) & (lane // HALF == m), light_ref[c, light], tint)
        mismatch = albedo * tint - targets[...]
        lg = (factor * mismatch * tint * albedo * (1.0 - albedo)).astype(BF)
        lgt = lg.astype(F32).T.astype(BF)
        og[...] = dot(lgt, hw).astype(BF)
        edges(2, og)
        halo_start(2, up, down)
        squares = jnp.sum(mismatch * mismatch)
        hg = dot(lg, o)
        row_h = lax.broadcasted_iota(jnp.int32, (8, CH), 0)
        hsum[0] = jnp.where(row_h == 3, squares, hg)

    sum_start(0)

    for m in range(MICROS):
        fill(cat_c, m, 2, og[tokens_of(m), :].astype(F32))

    def backward_halo():
        @pl.when(seg == 1)
        def _():
            halo_here(2)

        @pl.when(seg == 0)
        def _():
            halo_here(3)

        def rows_of(side, m):
            v = jnp.where(seg == 1, hrecv[2, side, m].astype(F32), hrecv[3, side, m].astype(F32))
            return v

        halo_rows(cat_c, rows_of)

    def through(m, row, n, v):
        h = hidden[m, row + 1 : row + 1 + n].reshape(n * COLS, CH)
        return (v * gelu_slope(h)).astype(BF).astype(F32)

    back = two_convs(cat_c, wflip, 1, through, cat_d, 0, backward_halo)
    for m in range(MICROS):
        rows = tokens_of(m)
        slope = gelu_slope(section_in[rows, :].astype(F32))
        grad[rows, :] = (og[rows, :].astype(F32) + back[m] * slope).astype(BF)

    @pl.when(seg == 1)
    def _():
        edges(3, grad)
        halo_start(3, up_other, down_other)
        seg_copy(grad, og_in, 1).start()

    sum_end(0)
    sum_start(1)

    def own_conv(slot, dp, r, dq):
        start = pl.multiple_of(slot * CSLOT, 8)
        return wf32[:, pl.ds(start, CSLOT), :]

    def own_proj(slot, dp, r, dq):
        return part[part_slot(dp, r, dq)]

    def store_conv(v):
        conv_out[...] = v

    def store_proj(v):
        proj_out[...] = v

    rc = Reduce(Axis(False), own_conv, store_conv, wconv, cgot, rcs, rcr)
    rp = Reduce(pa, own_proj, store_proj, wproj, pgot, rps, rpr, placed=True)

    def compute(dp, r):
        xs, ys, _ = pa.coords(dp, r, 0)
        base = xs * 8 + ys * 4
        lanes = pl.ds(pl.multiple_of(base * SLOT, CHUNK), CHUNK)
        v = dot(hooks_v[:, lanes], grad[...], ((0,), (0,)))
        for k in range(4):
            ahead = (k - z + 4) % 4
            block = v[k * SLOT : (k + 1) * SLOT]
            for dq in (0,) + ACROSS:

                @pl.when(ahead == dq % 4)
                def _():
                    if r == 1 and dp in SIDE:
                        wproj[side_slot(dp, dq)] = block.astype(BF)
                    elif dq == 0 or (r == 0 and dp in SIDE):
                        part[part_slot(dp, r, dq)] = block
                    else:
                        wproj[queue_slot(dp, r, dq)] = block.astype(BF)

    for i, (dp, r) in enumerate(BACK):
        compute(dp, r)
        rp.first(dp, r)
        if i == 2:

            @pl.when(seg == 1)
            def _():
                transposes()

            conv_weight_grad(x2t, cat_c, 3, 1)
            conv_weight_grad(x1t, cat_d, 2, 0)
            rc.first(*BACK[0])
            rc.first(*BACK[1])
        if i >= 2:
            rc.first(dp, r)
            if i < 7:
                sum_end(i - 1)
                if i < 6:
                    sum_start(i)
        if i >= 5:
            rc.second(*QUEUE[i - 5])
            rp.second(*QUEUE[i - 5])
    final = pltpu.make_async_remote_copy(
        src_ref=hsum.at[6],
        dst_ref=hfin,
        send_sem=seg_s.at[2],
        recv_sem=seg_r.at[2],
        device_id=sibling,
        device_id_type=MESH,
    )

    @pl.when(seg == 1)
    def _():
        final.start()
        total_ref[...] = hsum[6]

    for dp, r in QUEUE[3:]:
        rc.second(dp, r)
        rp.second(dp, r)
    rc.third()
    rp.third()
    rc.fourth()
    rp.fourth()
    halo_sent(0)

    @pl.when(seg == 1)
    def _():
        halo_sent(2)
        halo_sent(3)
        seg_copy(grad, og_in, 1).wait_send()
        final.wait_send()

    @pl.when(seg == 0)
    def _():
        final.wait_recv()
        total_ref[...] = hfin[...]


def run_main(factor, hooks, proj, conv, head, light, illum, offsets, photos):
    vm = pl.BlockSpec(memory_space=pltpu.VMEM)
    sm = pl.BlockSpec(memory_space=pltpu.SMEM)
    dma = pltpu.SemaphoreType.DMA
    field = pltpu.VMEM((TOKENS, CH), BF)
    return pl.pallas_call(
        functools.partial(main_kernel, factor),
        out_shape=(
            jax.ShapeDtypeStruct((SLOT, CH), F32),
            jax.ShapeDtypeStruct((2, CSLOT, CH), F32),
            jax.ShapeDtypeStruct((8, CH), F32),
        ),
        in_specs=[pl.BlockSpec(memory_space=pl.ANY), vm, vm, vm, sm, sm, sm, pl.BlockSpec(memory_space=pl.ANY)],
        out_specs=(vm, vm, vm),
        scratch_shapes=[
            pltpu.VMEM((TOKENS, D), BF),
            pltpu.VMEM((MICROS, 3, 96, 96), BF),
            pltpu.VMEM((32, SLOT, CH), BF),
            pltpu.VMEM((32, 2, CSLOT, CH), BF),
            pltpu.VMEM((2, 9 * CH, CH), F32),
            pltpu.VMEM((2, 9 * CH, CH), BF),
            pltpu.VMEM((2, 9 * CH, CH), BF),
            pltpu.VMEM((TOKENS, CH), F32),
            field,
            field,
            field,
            field,
            field,
            field,
            pltpu.VMEM((MICROS, ROWS + 2, COLS, CH), F32),
            pltpu.VMEM((MICROS, ROWS + 4, COLS, 3 * CH), BF),
            pltpu.VMEM((MICROS, ROWS + 2, COLS, 3 * CH), BF),
            pltpu.VMEM((MICROS, ROWS + 4, COLS, 3 * CH), BF),
            pltpu.VMEM((MICROS, ROWS + 2, COLS, 3 * CH), BF),
            pltpu.VMEM((CH, TOKENS), BF),
            pltpu.VMEM((CH, TOKENS), BF),
            pltpu.VMEM((4, 2, MICROS, 2 * COLS, CH), BF),
            pltpu.VMEM((4, 2, MICROS, 2 * COLS, CH), BF),
            pltpu.VMEM((8, TOKENS), F32),
            pltpu.VMEM((8, CH), F32),
            pltpu.VMEM((7, 8, CH), F32),
            pltpu.VMEM((6, 8, CH), F32),
            pltpu.VMEM((8, CH), F32),
            pltpu.VMEM((12, SLOT, CH), F32),
            pltpu.VMEM((32, SLOT, CH), BF),
            pltpu.VMEM((32, 2, CSLOT, CH), BF),
            dma((8 + MICROS,)),
            dma((32,)),
            dma((32,)),
            dma((32,)),
            dma((32,)),
            dma((4, 2)),
            dma((4, 2)),
            dma((3,)),
            dma((3,)),
            dma((6,)),
            dma((6,)),
            dma((32,)),
            dma((32,)),
            dma((32,)),
            dma((32,)),
            pltpu.SemaphoreType.REGULAR,
        ],
        compiler_params=pltpu.CompilerParams(
            collective_id=0, has_side_effects=True, vmem_limit_bytes=60 * 1024 * 1024
        ),
        cost_estimate=pl.CostEstimate(
            flops=15_000_000_000, bytes_accessed=14_000_000, transcendentals=1_000_000
        ),
        name="main_kernel",
    )(hooks, proj, conv, head, light, illum, offsets, photos)


def finish_kernel(npix, proj_ref, conv_ref, total_ref, proj_out, conv_out, head_out, loss_out):
    proj_out[...] = proj_ref[...]
    conv_out[...] = conv_ref[...]
    head_out[...] = total_ref[0:3, :]
    loss_out[...] = total_ref[3:4, 0:1] / npix


def run_finish(npix, proj, conv, total):
    vm = pl.BlockSpec(memory_space=pltpu.VMEM)
    return pl.pallas_call(
        functools.partial(finish_kernel, npix),
        out_shape=(
            jax.ShapeDtypeStruct((SLOT, CH), F32),
            jax.ShapeDtypeStruct((2, CSLOT, CH), F32),
            jax.ShapeDtypeStruct((3, CH), F32),
            jax.ShapeDtypeStruct((1, 1), F32),
        ),
        in_specs=[vm, vm, vm],
        out_specs=(vm, vm, vm, vm),
        name="finish_kernel",
    )(proj, conv, total)


def body(hooks, proj_weight, conv_weight, head_weight, light_color, illum, offsets, photos):
    npix = 3 * MICROS * lax.axis_size("dp") * ROWS * lax.axis_size("fsdp") * COLS
    factor = 2.0 * LOSS_SCALE / npix
    tokens = hooks.reshape(TOKENS, D)
    grad_proj, grad_conv, total = run_main(
        factor, tokens, proj_weight[0], conv_weight[0], head_weight, light_color.T,
        illum, offsets.transpose(0, 2, 1), photos,
    )
    grad_proj, grad_conv, head, loss = run_finish(npix, grad_proj, grad_conv, total)
    return (grad_proj[None], grad_conv[None], head, loss[0, 0])


def solution(mesh):
    placed = (
        P("segment", "dp", "fsdp", None, None),
        P("segment", "fsdp", None),
        P("segment", None, "fsdp", None),
        P(),
        P(),
        P("dp", None),
        P("dp", None, None),
        P("dp", None, None, None, None),
    )
    return jax.shard_map(
        body,
        mesh=mesh,
        in_specs=placed,
        out_specs=(P("segment", "fsdp", None), P("segment", None, "fsdp", None), P(), P()),
        check_vma=False,
    )
```
